128 devices in a mesh: seq: 16 (over y, x), mp: 8 (over z, core).
Axes of the slice: x: 4, y: 4, z: 4, core: 2. Of those that a mesh axis runs over, the one named last changes fastest.
Arguments:
- tokens: bfloat16 [8192, 8192], P('seq', 'mp'), may hold values from -26 to 26
- query_weight: bfloat16 [8192, 4096], P('mp', 'seq'), may hold values from -0.0625 to 0.0625
- key_value_matrix: bfloat16 [8192, 1024], P('mp'), may hold values from -0.0625 to 0.0625
- output_weight: bfloat16 [4096, 8192], P(None, 'mp'), may hold values from -0.09375 to 0.09375
- document_lengths: int32 [16], replicated, may hold values from 1 to 2048, 8192 in all
- block_order: int32 [64], replicated, may hold values from 0 to 63, each once
Outputs:
- layer_out: bfloat16 [8192, 8192], P('seq', 'mp')
The draws below stay inside these ranges and needn't reach their ends.
Inputs may be any that keep to these rules, and one draw needn't show every extreme that they name: `document_lengths`: they sum to 8192; the longest document has exactly 2048 tokens. A permutation: row block b of the layout (rows b * 128 to b * 128 + 127) holds the window positions block_order[b] * 128 onward, in order.
All inputs are finite; a program needn't handle non-finite values.
Results may differ from the reference program's by a relative error of at most 0.034.
Values may be sent and summed in bfloat16 or wider, within the bound.
A program may use at most 128 MiB of HBM per device.

```python
import math
import jax
import jax.numpy as jnp
import numpy as np
from jax import lax

MODEL_WIDTH = 8192
QUERY_HEADS = 32
KEY_VALUE_HEADS = 4
HEAD_SIZE = 128
BLK = 128
NDOC = 16
WINDOW_TOKENS = 8192
NBLK = 64
N_MP = 8


def draw_tokens(key, part):
    value_matrix = jnp.clip(jax.random.normal(key, (WINDOW_TOKENS, MODEL_WIDTH), jnp.float32), -6.0, 6.0)
    return jnp.clip(value_matrix, -26.0, 26.0).astype(jnp.bfloat16)


def shard_levels(own_key, dims, cuts, least, high):
    level, own = 1.0, jax.random.fold_in(own_key, 6)
    for position, blocks in cuts:
        heights = jnp.exp(jax.random.uniform(jax.random.fold_in(own, position), (blocks,), jnp.float32, least / len(cuts), high / len(cuts)))
        level = level * jnp.repeat(heights, dims[position] // blocks).reshape([-1 if axis == position else 1 for axis in range(len(dims))])
    return level


def profile(number_of, total, reach, slope):
    loads = [(1 << 20) // math.isqrt(rank ** slope) + 1 for rank in range(2, number_of + 1)]
    surplus, holding = total - reach - (number_of - 1), [1] * (number_of - 1)
    while surplus > 0:
        free = [i for i in range(number_of - 1) if holding[i] < reach]
        pool, remaining = sum([loads[i] for i in free]), surplus
        for i in free:
            extra = min(reach - holding[i], max(1, remaining * loads[i] // pool), surplus)
            holding[i] = holding[i] + extra
            surplus = surplus - extra
    return np.array([reach] + holding)


def uneven_parts(key, number_of, total, bound, slope):
    if number_of == 2:
        one = jax.random.randint(key, (), max(1, total - bound), min(bound, total - 1) + 1)
        return jnp.stack([one, total - one])
    sizes = jnp.asarray(profile(number_of, total, bound, slope), jnp.int32)
    couples = (number_of - 1) // 2
    donor, receiver = sizes[1:1 + 2 * couples:2], sizes[2:2 + 2 * couples:2]
    margin = jnp.minimum(donor - 1, bound - receiver)
    shifted = jax.random.randint(jax.random.fold_in(key, 1), (couples,), 0, 1 << 20) % (margin + 1)
    sizes = sizes.at[1:1 + 2 * couples:2].set(donor - shifted).at[2:2 + 2 * couples:2].set(receiver + shifted)
    return sizes[jax.random.permutation(jax.random.fold_in(key, 2), number_of)]


def noise(rng, shape, spread, limit, shards=(), held_as=jnp.bfloat16):
    loudness = shard_levels(rng, shape, shards, -0.22, 0.18) if shards else 1.0
    entries = jax.random.normal(rng, shape, jnp.float32) * spread * loudness
    return jnp.minimum(jnp.maximum(entries, -limit), limit).astype(held_as)


def setup_inputs(seed: int = 0) -> dict:
    key_of = jax.random.split(jax.random.key(seed), 7)
    return {
        "tokens": draw_tokens(jax.random.fold_in(key_of[6], 71), 0),
        "query_weight": noise(key_of[1], (MODEL_WIDTH, QUERY_HEADS * HEAD_SIZE), MODEL_WIDTH ** -0.5, 0.0625, ((0, 8), (1, 16))),
        "key_value_matrix": noise(key_of[2], (MODEL_WIDTH, 2 * KEY_VALUE_HEADS * HEAD_SIZE), MODEL_WIDTH ** -0.5, 0.0625, ((0, 8),)),
        "output_weight": noise(key_of[3], (QUERY_HEADS * HEAD_SIZE, MODEL_WIDTH), (QUERY_HEADS * HEAD_SIZE) ** -0.5, 0.09375, ((1, 8),)),
        "document_lengths": uneven_parts(key_of[4], NDOC, WINDOW_TOKENS, WINDOW_TOKENS // 4, 2).astype(jnp.int32),
        "block_order": jax.random.permutation(key_of[5], NBLK).astype(jnp.int32),
    }


rope_base = 500000.0
neg_large = -1e+30

def round_term(term_f32):
    return lax.optimization_barrier(term_f32.astype(jnp.bfloat16)).astype(jnp.float32)

def rotary_pair_turn(value_matrix, token_positions):
    row_count = value_matrix.shape[0]
    shaped = value_matrix.reshape(row_count, -1, HEAD_SIZE)
    half_dim = HEAD_SIZE // 2
    inverse = jnp.exp(-(2.0 * jnp.arange(half_dim, dtype=jnp.float32) / HEAD_SIZE) * jnp.log(jnp.float32(rope_base)))
    angles = token_positions.astype(jnp.float32)[:, None] * inverse[None, :]
    cosine = jnp.cos(angles)[:, None, :]
    sine_part = jnp.sin(angles)[:, None, :]
    first_half = shaped[..., :half_dim]
    second_half = shaped[..., half_dim:]
    turned = jnp.concatenate([first_half * cosine - second_half * sine_part, second_half * cosine + first_half * sine_part], axis=-1)
    return turned.reshape(row_count, -1)

def place_rows(row_ids, block_order):
    blocks = block_order.shape[0]
    lookup = jnp.where((row_ids // BLK)[:, None] == jnp.arange(blocks, dtype=jnp.int32)[None, :], block_order[None, :], 0)
    return (lax.optimization_barrier(jnp.sum(lookup, axis=1)) * BLK + row_ids % BLK).astype(jnp.int32)

def owner_of(token_positions, document_lengths):
    doc_ends = jnp.cumsum(document_lengths).astype(jnp.int32)
    return lax.optimization_barrier(jnp.sum((doc_ends[None, :] <= token_positions[:, None]).astype(jnp.int32), axis=1))

def reference(tokens, query_weight, key_value_matrix, output_weight, document_lengths, block_order):
    slice_width = MODEL_WIDTH // N_MP
    query_sum = jnp.zeros((WINDOW_TOKENS, QUERY_HEADS * HEAD_SIZE), jnp.float32)
    pairwise_sum = jnp.zeros((WINDOW_TOKENS, 2 * KEY_VALUE_HEADS * HEAD_SIZE), jnp.float32)
    for member in range(N_MP):
        low = member * slice_width
        high = low + slice_width
        picked = tokens[:, low:high]
        query_sum = query_sum + round_term(jnp.dot(picked, query_weight[low:high], preferred_element_type=jnp.float32))
        pairwise_sum = pairwise_sum + round_term(jnp.dot(picked, key_value_matrix[low:high], preferred_element_type=jnp.float32))
    row_ids = jnp.arange(WINDOW_TOKENS, dtype=jnp.int32)
    token_positions = place_rows(row_ids, block_order)
    documents = owner_of(token_positions, document_lengths)
    queries = rotary_pair_turn(query_sum, token_positions).astype(jnp.bfloat16)
    key_row_block = rotary_pair_turn(pairwise_sum[:, :KEY_VALUE_HEADS * HEAD_SIZE], token_positions).astype(jnp.bfloat16)
    value_matrix = pairwise_sum[:, KEY_VALUE_HEADS * HEAD_SIZE:].astype(jnp.bfloat16)
    query_heads = queries.reshape(WINDOW_TOKENS, QUERY_HEADS, HEAD_SIZE).transpose(1, 0, 2)
    key_head_rows = key_row_block.reshape(WINDOW_TOKENS, KEY_VALUE_HEADS, HEAD_SIZE).transpose(1, 0, 2)
    value_head_rows = value_matrix.reshape(WINDOW_TOKENS, KEY_VALUE_HEADS, HEAD_SIZE).transpose(1, 0, 2)
    tile_rows = 1024 if WINDOW_TOKENS % 1024 == 0 else WINDOW_TOKENS
    score_scale = 1.0 / math.sqrt(HEAD_SIZE)

    def one_head(head_total):
        query_one = lax.dynamic_index_in_dim(query_heads, head_total, 0, keepdims=False)
        common_key_head = head_total // (QUERY_HEADS // KEY_VALUE_HEADS)
        key_one = lax.dynamic_index_in_dim(key_head_rows, common_key_head, 0, keepdims=False)
        value_one = lax.dynamic_index_in_dim(value_head_rows, common_key_head, 0, keepdims=False)

        def one_block(number):
            offset = number * tile_rows
            query_block = lax.dynamic_slice_in_dim(query_one, offset, tile_rows, 0)
            block_position = lax.dynamic_slice_in_dim(token_positions, offset, tile_rows, 0)
            block_document = lax.dynamic_slice_in_dim(documents, offset, tile_rows, 0)
            scores = jnp.dot(query_block, key_one.T, preferred_element_type=jnp.float32) * score_scale
            allowed = (block_document[:, None] == documents[None, :]) & (token_positions[None, :] <= block_position[:, None])
            largest = lax.optimization_barrier(jnp.max(jnp.where(allowed, scores, neg_large), axis=1, keepdims=True))
            weights = jnp.where(allowed, jnp.exp(scores - largest), 0.0).astype(jnp.bfloat16)
            denominator = lax.optimization_barrier(jnp.sum(weights.astype(jnp.float32), axis=1, keepdims=True))
            mixed_out = jnp.dot(weights, value_one, preferred_element_type=jnp.float32) / denominator
            return mixed_out.astype(jnp.bfloat16)
        return lax.map(one_block, jnp.arange(WINDOW_TOKENS // tile_rows, dtype=jnp.int32)).reshape(WINDOW_TOKENS, HEAD_SIZE)
    attended = lax.map(one_head, jnp.arange(QUERY_HEADS, dtype=jnp.int32))
    attended = attended.transpose(1, 0, 2).reshape(WINDOW_TOKENS, QUERY_HEADS * HEAD_SIZE)
    return jnp.dot(attended, output_weight, preferred_element_type=jnp.float32).astype(jnp.bfloat16)
```

```python
import functools
import math

import jax
import jax.numpy as jnp
import numpy as np
from jax import lax
from jax.experimental import pallas as pl
from jax.experimental.pallas import tpu as pltpu
from jax.sharding import PartitionSpec as P

MESH = pl.DeviceIdType.MESH
HEAD = 128
BLK = 128
ROWS = 512
WIDTH = 1024
WINDOW_BLOCKS = 17
ROPE_BASE = 500000.0
NEG = -1e30
BF16 = jnp.bfloat16
F32 = jnp.float32


def rope_tables():
    half = HEAD // 2
    inverse = np.exp(-(2.0 * np.arange(half) / HEAD) * np.log(ROPE_BASE))
    within = np.arange(BLK)[:, None] * inverse[None, :]
    start = (np.arange(64) * BLK)[:, None] * inverse[None, :]

    def both(values, sign):
        return np.concatenate([sign * values, values], axis=1).astype(np.float32)

    return (
        both(np.cos(within), 1.0),
        both(np.sin(within), -1.0),
        both(np.cos(start), 1.0),
        both(np.sin(start), -1.0),
    )


def place():
    s = lax.axis_index("seq")
    m = lax.axis_index("mp")
    return s // 4, s % 4, m // 2, m % 2


def at(y, x, z, c, dy=0, dx=0, dz=0, dc=0):
    return (((y + dy) % 4) * 4 + (x + dx) % 4, ((z + dz) % 4) * 2 + (c + dc) % 2)


def greet(here, offsets):
    barrier = pltpu.get_barrier_semaphore()
    for off in offsets:
        pl.semaphore_signal(barrier, inc=1, device_id=at(*here, **off), device_id_type=MESH)
    pl.semaphore_wait(barrier, len(offsets))


class Copies:
    def __init__(self, here, send, recv):
        self.here, self.send, self.recv = here, send, recv
        self.count, self.open = 0, []

    def start(self, src, dst, **off):
        k = self.count
        self.count += 1
        copy = pltpu.make_async_remote_copy(
            src_ref=src,
            dst_ref=dst,
            send_sem=self.send.at[k],
            recv_sem=self.recv.at[k],
            device_id=at(*self.here, **off),
            device_id_type=MESH,
        )
        copy.start()
        self.open.append(copy)
        return copy

    def drain(self):
        for copy in self.open:
            copy.wait_send()


def turn(values, block, tables):
    cr, sr, cb, sb = tables
    c0 = cb[pl.ds(block, 1), :]
    s0 = sb[pl.ds(block, 1), :]
    cosine = c0 * cr[...] - s0 * sr[...]
    sine = s0 * cr[...] + c0 * sr[...]
    return values * cosine + pltpu.roll(values, HEAD // 2, 1) * sine


N_K1 = 55
ALL_OFFSETS = [
    dict(dx=1),
    dict(dx=3),
    dict(dx=2),
    dict(dy=1),
    dict(dy=3),
    dict(dz=1),
    dict(dz=3),
    dict(dz=2),
    dict(dc=1),
]


def project_kernel(
    order, cr, sr, cb, sb, tok, wq, wkv, q_out, kv,
    tx, wy, kv_mine, kv_sib_s, kv_sib_r, kv_z_s, kv_z_r,
    q_mine, q_own, q_sib_s, q_sib_r, q_z_s, q_z_r, send, recv,
):
    here = place()
    y, x, z, c = here
    s = 4 * y + x
    tables = (cr, sr, cb, sb)
    greet(here, ALL_OFFSETS)
    go = Copies(here, send, recv)
    top, low = pl.ds(0, ROWS // 2), pl.ds(ROWS // 2, ROWS // 2)
    wtop, wlow = pl.ds(0, WIDTH // 2), pl.ds(WIDTH // 2, WIDTH // 2)

    w_up_t = go.start(wq.at[wtop], wy.at[y, wtop], dy=1)
    w_dn_l = go.start(wq.at[wlow], wy.at[y, wlow], dy=3)
    t_up_t = go.start(tok.at[top], tx.at[0, top], dx=1)
    t_dn_l = go.start(tok.at[low], tx.at[1, low], dx=3)
    w_up_l = go.start(wq.at[wlow], wy.at[y, wlow], dy=1)
    w_dn_t = go.start(wq.at[wtop], wy.at[y, wtop], dy=3)
    t_up_l = go.start(tok.at[low], tx.at[0, low], dx=1)
    t_dn_t = go.start(tok.at[top], tx.at[1, top], dx=3)

    def pair_part(half, out):
        rows = tok[pl.ds(pl.multiple_of(half * 256, 256), 256), :]
        for g in range(4):
            part = jnp.dot(rows, wkv[:, pl.ds(g * 256, 256)], preferred_element_type=F32)
            for i in range(2):
                h = 2 * g + i
                out[h % 4, :, pl.ds((h // 4) * HEAD, HEAD)] = part[:, i * HEAD : (i + 1) * HEAD].astype(out.dtype)

    pair_part(1 - c, kv_sib_s)
    sib = go.start(kv_sib_s, kv_sib_r, dc=1)
    pair_part(c, kv_mine)
    wy[y] = wq[...]
    sib.wait_recv()
    kv_z = []
    for r in (2, 1, 3):
        d = (z + r) % 4
        kv_z_s[r - 1] = (kv_mine[d] + kv_sib_r[d].astype(F32)).astype(BF16)
        kv_z.append(go.start(kv_z_s.at[r - 1], kv_z_r.at[r - 1], dz=r))
    own_pair = kv_mine[z] + kv_sib_r[z].astype(F32)
    for copy in kv_z:
        copy.wait_recv()
    for r in range(3):
        own_pair = own_pair + kv_z_r[r].astype(F32)
    kv[c, s, :, pl.ds(HEAD, HEAD)] = own_pair[:, HEAD:].astype(BF16)
    for i in range(2):
        block = order[4 * s + 2 * c + i]
        part = own_pair[i * BLK : (i + 1) * BLK, :HEAD]
        kv[c, s, pl.ds(i * BLK, BLK), pl.ds(0, HEAD)] = turn(part, block, tables).astype(BF16)
    kv_x = [go.start(kv.at[c, s], kv.at[c, s], dx=r) for r in (2, 1, 3)]

    w_up_t.wait_recv()
    w_rel_up = go.start(wy.at[(y + 3) % 4, wtop], wy.at[(y + 3) % 4, wtop], dy=1)
    w_dn_l.wait_recv()
    w_rel_dn = go.start(wy.at[(y + 1) % 4, wlow], wy.at[(y + 1) % 4, wlow], dy=3)
    for copy in (w_up_l, w_dn_t, w_rel_up, w_rel_dn):
        copy.wait_recv()

    def project(rows, t):
        def one(g, carry):
            part = jnp.dot(rows[...], wy[g], preferred_element_type=F32)
            first, second = part[:, :HEAD], part[:, HEAD:]
            q_mine[g] = jnp.where(c == 0, first, second)
            q_sib_s[t, g] = jnp.where(c == 0, second, first).astype(BF16)
            return carry

        lax.fori_loop(0, 4, one, 0)
        return go.start(q_sib_s.at[t], q_sib_r.at[t], dc=1)

    def spread(t, copy):
        copy.wait_recv()
        sent = []
        for r in (2, 1, 3):
            d = (z + r) % 4
            q_z_s[t, r - 1] = (q_mine[d] + q_sib_r[t, d].astype(F32)).astype(BF16)
            sent.append(go.start(q_z_s.at[t, r - 1], q_z_r.at[t, r - 1], dz=r))
        q_own[t] = q_mine[z] + q_sib_r[t, z].astype(F32)
        return sent

    scale = math.log2(math.e) / math.sqrt(HEAD)

    def finish(t, shift, sent):
        for copy in sent:
            copy.wait_recv()
        first = 4 * (4 * y + (x + shift) % 4)
        for i in range(4):
            rows = pl.ds(i * BLK, BLK)
            total = q_own[t, rows, :]
            for r in range(3):
                total = total + q_z_r[t, r, rows, :].astype(F32)
            q_out[t, rows, :] = (turn(total, order[first + i], tables) * scale).astype(BF16)

    own_sent = spread(0, project(tok, 0))

    for copy in kv_x:
        copy.wait_recv()
    row = kv.at[c, pl.ds(4 * y, 4)]
    kv_up = go.start(row, row, dy=1)
    kv_dn = go.start(row, row, dy=3)
    kv_sib = [go.start(row, row, dc=1)]

    t_up_t.wait_recv()
    t_rel_up = go.start(tx.at[0, top], tx.at[2, top], dx=1)
    t_dn_l.wait_recv()
    t_rel_dn = go.start(tx.at[1, low], tx.at[2, low], dx=3)
    finish(0, 0, own_sent)
    t_up_l.wait_recv()
    left_sent = spread(1, project(tx.at[0], 1))
    t_dn_t.wait_recv()
    right_sent = spread(2, project(tx.at[1], 2))

    kv_up.wait_recv()
    part = kv.at[c, pl.ds(4 * ((y + 3) % 4), 2)]
    kv_rel_up = go.start(part, part, dy=1)
    kv_dn.wait_recv()
    part = kv.at[c, pl.ds(4 * ((y + 1) % 4) + 2, 2)]
    kv_rel_dn = go.start(part, part, dy=3)
    for r in (1, 3):
        row = kv.at[c, pl.ds(4 * ((y + r) % 4), 4)]
        kv_sib.append(go.start(row, row, dc=1))
    finish(1, 3, left_sent)
    finish(2, 1, right_sent)
    t_rel_up.wait_recv()
    t_rel_dn.wait_recv()
    far_sent = spread(3, project(tx.at[2], 3))
    kv_rel_up.wait_recv()
    kv_rel_dn.wait_recv()
    row = kv.at[c, pl.ds(4 * ((y + 2) % 4), 4)]
    kv_sib.append(go.start(row, row, dc=1))
    finish(3, 2, far_sent)
    for copy in kv_sib:
        copy.wait_recv()
    go.drain()


def project(order, tok, wq, wkv):
    vm = pl.BlockSpec(memory_space=pltpu.VMEM)
    sm = pl.BlockSpec(memory_space=pltpu.SMEM)
    n = 55
    return pl.pallas_call(
        project_kernel,
        out_shape=(
            jax.ShapeDtypeStruct((4, ROWS, HEAD), BF16),
            jax.ShapeDtypeStruct((2, 16, 256, 256), BF16),
        ),
        in_specs=[sm] + [vm] * 7,
        out_specs=(vm, vm),
        scratch_shapes=[
            pltpu.VMEM((3, ROWS, WIDTH), BF16),
            pltpu.VMEM((4, WIDTH, 256), BF16),
            pltpu.VMEM((4, 256, 256), F32),
            pltpu.VMEM((4, 256, 256), BF16),
            pltpu.VMEM((4, 256, 256), BF16),
            pltpu.VMEM((3, 256, 256), BF16),
            pltpu.VMEM((3, 256, 256), BF16),
            pltpu.VMEM((4, ROWS, HEAD), F32),
            pltpu.VMEM((4, ROWS, HEAD), F32),
            pltpu.VMEM((4, 4, ROWS, HEAD), BF16),
            pltpu.VMEM((4, 4, ROWS, HEAD), BF16),
            pltpu.VMEM((4, 3, ROWS, HEAD), BF16),
            pltpu.VMEM((4, 3, ROWS, HEAD), BF16),
            pltpu.SemaphoreType.DMA((n,)),
            pltpu.SemaphoreType.DMA((n,)),
        ],
        compiler_params=pltpu.CompilerParams(
            collective_id=0, has_side_effects=True, vmem_limit_bytes=48 << 20
        ),
    )(order, *[jnp.asarray(t) for t in rope_tables()], tok, wq, wkv)


def attend_kernel(order, where, lengths, q, kv, out, score):
    y, x, z, c = place()

    def one(n, carry):
        t, i = n // 4, n % 4
        shift = jnp.where(t == 0, 0, jnp.where(t == 1, 3, jnp.where(t == 2, 1, 2)))
        block = order[4 * (4 * y + (x + shift) % 4) + i]
        rows = pl.ds(pl.multiple_of(i * BLK, BLK), BLK)
        query = q[t, rows, :]
        pos = lax.broadcasted_iota(jnp.int32, (BLK, BLK), 0) + block * BLK
        lane = lax.broadcasted_iota(jnp.int32, (BLK, BLK), 1)
        begin = jnp.zeros((BLK, BLK), jnp.int32)
        end = jnp.int32(0)
        for d in range(16):
            end = end + lengths[d]
            begin = jnp.where(pos >= end, end, begin)
        base = (block - (WINDOW_BLOCKS - 1)) * BLK
        ahead = lane + (base - begin)
        top = jnp.full((BLK, BLK), NEG, F32)
        offsets = []
        for j in range(WINDOW_BLOCKS):
            held = where[jnp.maximum(block - (WINDOW_BLOCKS - 1) + j, 0)]
            off = (held % 4) // 2 * 4096 + held // 4 * 256 + held % 2 * 128
            off = pl.multiple_of(off, 128)
            offsets.append(off)
            keys = kv[pl.ds(off, BLK), pl.ds(0, HEAD)]
            s = lax.dot_general(query, keys, (((1,), (1,)), ((), ())), preferred_element_type=F32)
            allowed = ahead >= -j * BLK
            if j == WINDOW_BLOCKS - 1:
                allowed = allowed & (lane <= pos - block * BLK)
            s = jnp.where(allowed, s, NEG)
            score[j] = s
            top = jnp.maximum(top, s)
        largest = jnp.max(top, axis=1, keepdims=True)
        total = jnp.zeros((BLK, BLK), F32)
        acc = jnp.zeros((BLK, HEAD), F32)
        for j in range(WINDOW_BLOCKS):
            w = jnp.exp2(score[j] - largest)
            total = total + w
            values = kv[pl.ds(offsets[j], BLK), pl.ds(HEAD, HEAD)]
            acc = acc + jnp.dot(w.astype(BF16), values, preferred_element_type=F32)
        out[t, rows, :] = (acc / jnp.sum(total, axis=1, keepdims=True)).astype(BF16)
        return carry

    lax.fori_loop(0, 16, one, 0)


def attend(order, where, lengths, q, kv):
    vm = pl.BlockSpec(memory_space=pltpu.VMEM)
    sm = pl.BlockSpec(memory_space=pltpu.SMEM)
    return pl.pallas_call(
        attend_kernel,
        out_shape=jax.ShapeDtypeStruct((4, ROWS, HEAD), BF16),
        in_specs=[sm, sm, sm, vm, vm],
        out_specs=vm,
        scratch_shapes=[pltpu.VMEM((WINDOW_BLOCKS, BLK, BLK), F32)],
        compiler_params=pltpu.CompilerParams(vmem_limit_bytes=32 << 20),
    )(order, where, lengths, q, kv.reshape(8192, 256))


OUT_OFFSETS = [
    dict(dx=1),
    dict(dx=3),
    dict(dx=2),
    dict(dz=1),
    dict(dz=3),
    dict(dz=2),
    dict(dc=1),
]


def output_kernel(a, wo_hbm, out, att, wo, acc, local, send, recv):
    here = place()
    y, x, z, c = here
    load = pltpu.make_async_copy(wo_hbm, wo, local)
    load.start()
    greet(here, OUT_OFFSETS)
    go = Copies(here, send, recv)
    home = [
        go.start(a.at[1], att.at[z, c, x], dx=3),
        go.start(a.at[2], att.at[z, c, x], dx=1),
        go.start(a.at[3], att.at[z, c, x], dx=2),
    ]
    att[z, c, x] = a[0]
    lifts = []
    for k, shift in enumerate((0, 1, 3, 2)):
        if k:
            home[k - 1].wait_recv()
        piece = att.at[z, c, (x + shift) % 4]
        lifts.append([go.start(piece, piece, dz=r) for r in (2, 1, 3)])
    sib = [go.start(att.at[z, c], att.at[z, c], dc=1)]
    load.wait()

    def multiply(d, first):
        heads = [att[d, i % 2, i // 2] for i in range(8)]
        left = jnp.concatenate(heads, axis=1)
        depth = pl.ds(pl.multiple_of(d * WIDTH, WIDTH), WIDTH)

        def tile(n, carry):
            cols = pl.ds(pl.multiple_of(n * 256, 256), 256)
            part = jnp.dot(left, wo[depth, cols], preferred_element_type=F32)
            acc[:, cols] = part if first else acc[:, cols] + part
            return carry

        lax.fori_loop(0, 4, tile, 0)

    sib[0].wait_recv()
    multiply(z, True)
    for i, r in ((1, 1), (2, 3), (0, 2)):
        d = (z + 4 - r) % 4
        for lift in lifts:
            lift[i].wait_recv()
        copy = go.start(att.at[d, c], att.at[d, c], dc=1)
        copy.wait_recv()
        multiply(d, False)
    out[...] = acc[...].astype(BF16)
    go.drain()


def project_out(a, wo):
    vm = pl.BlockSpec(memory_space=pltpu.VMEM)
    n = 19
    return pl.pallas_call(
        output_kernel,
        out_shape=jax.ShapeDtypeStruct((ROWS, WIDTH), BF16),
        in_specs=[vm, pl.BlockSpec(memory_space=pl.ANY)],
        out_specs=vm,
        scratch_shapes=[
            pltpu.VMEM((4, 2, 4, ROWS, HEAD), BF16),
            pltpu.VMEM((4 * WIDTH, WIDTH), BF16),
            pltpu.VMEM((ROWS, WIDTH), F32),
            pltpu.SemaphoreType.DMA,
            pltpu.SemaphoreType.DMA((n,)),
            pltpu.SemaphoreType.DMA((n,)),
        ],
        compiler_params=pltpu.CompilerParams(
            collective_id=1, has_side_effects=True, vmem_limit_bytes=32 << 20
        ),
    )(a, wo)


def body(tokens, query_weight, key_value_matrix, output_weight, document_lengths, block_order):
    blocks = jnp.arange(64, dtype=jnp.int32)
    where = jnp.sum(jnp.where(block_order[None, :] == blocks[:, None], blocks[None, :], 0), axis=1)
    q, kv = project(block_order, tokens, query_weight, key_value_matrix)
    a = attend(block_order, where, document_lengths, q, kv)
    return project_out(a, output_weight)


def solution(mesh):
    placed = (P("seq", "mp"), P("mp", "seq"), P("mp", None), P(None, "mp"), P(), P())
    return jax.shard_map(
        body, mesh=mesh, in_specs=placed, out_specs=P("seq", "mp"), check_vma=False
    )
```

```python
import functools
import math

import jax
import jax.numpy as jnp
import numpy as np
from jax import lax
from jax.experimental import pallas as pl
from jax.experimental.pallas import tpu as pltpu
from jax.sharding import PartitionSpec as P

MESH = pl.DeviceIdType.MESH
HEAD = 128
BLK = 128
ROWS = 512
WIDTH = 1024
WINDOW_BLOCKS = 17
ROPE_BASE = 500000.0
NEG = -1e30
BF16 = jnp.bfloat16
F32 = jnp.float32


UNITS = ((0, 0), (0, 1), (1, 0), (2, 1), (1, 1), (2, 0), (3, 0), (3, 1))
SHIFT = (0, 3, 1, 2)
HALF = ROWS // 2


def rope_tables():
    half = HEAD // 2
    inverse = np.exp(-(2.0 * np.arange(half) / HEAD) * np.log(ROPE_BASE))
    within = np.arange(BLK)[:, None] * inverse[None, :]
    start = (np.arange(64) * BLK)[:, None] * inverse[None, :]

    def both(values, sign):
        return np.concatenate([sign * values, values], axis=1).astype(np.float32)

    return np.concatenate(
        [
            both(np.cos(within), 1.0),
            both(np.sin(within), -1.0),
            both(np.cos(start), 1.0),
            both(np.sin(start), -1.0),
        ]
    )


def place():
    s = lax.axis_index("seq")
    m = lax.axis_index("mp")
    return s // 4, s % 4, m // 2, m % 2


def at(y, x, z, c, dy=0, dx=0, dz=0, dc=0):
    return (((y + dy) % 4) * 4 + (x + dx) % 4, ((z + dz) % 4) * 2 + (c + dc) % 2)


def greet(here, offsets):
    barrier = pltpu.get_barrier_semaphore()
    for off in offsets:
        pl.semaphore_signal(barrier, inc=1, device_id=at(*here, **off), device_id_type=MESH)
    pl.semaphore_wait(barrier, len(offsets))


class Copies:
    def __init__(self, here, send, recv):
        self.here, self.send, self.recv = here, send, recv
        self.count, self.open = 0, []

    def start(self, src, dst, **off):
        k = self.count
        self.count += 1
        copy = pltpu.make_async_remote_copy(
            src_ref=src,
            dst_ref=dst,
            send_sem=self.send.at[k],
            recv_sem=self.recv.at[k],
            device_id=at(*self.here, **off),
            device_id_type=MESH,
        )
        copy.start()
        self.open.append(copy)
        return copy

    def drain(self):
        for copy in self.open:
            copy.wait_send()


def turn(values, block, table):
    cr, sr = table[pl.ds(0, BLK), :], table[pl.ds(BLK, BLK), :]
    c0 = table[pl.ds(2 * BLK + block, 1), :]
    s0 = table[pl.ds(2 * BLK + 64 + block, 1), :]
    cosine = c0 * cr - s0 * sr
    sine = s0 * cr + c0 * sr
    return values * cosine + pltpu.roll(values, HEAD // 2, 1) * sine


OFFSETS = [
    dict(dx=1),
    dict(dx=3),
    dict(dx=2),
    dict(dy=1),
    dict(dy=3),
    dict(dz=1),
    dict(dz=3),
    dict(dz=2),
    dict(dc=1),
]


def layer_kernel(
    order, where, lengths, table_hbm, tok_hbm, wq, wkv_hbm, wo_hbm, out,
    table, tok, wkv, wo, tx, wy, kv, kv_mine, kv_sib_s, kv_sib_r, kv_z_s, kv_z_r,
    q_mine, q_sib_s, q_sib_r, q_z_s, q_z_r, q, score, away, att, acc, local, send, recv,
):
    here = place()
    y, x, z, c = here
    s = 4 * y + x
    loads = [
        pltpu.make_async_copy(src, dst, local.at[k])
        for k, (src, dst) in enumerate(
            ((tok_hbm, tok), (wkv_hbm, wkv), (table_hbm, table), (wq, wy.at[y]), (wo_hbm, wo))
        )
    ]
    for load in loads:
        load.start()
    greet(here, OFFSETS)
    go = Copies(here, send, recv)
    top, low = pl.ds(0, HALF), pl.ds(HALF, HALF)
    wtop, wlow = pl.ds(0, WIDTH // 2), pl.ds(WIDTH // 2, WIDTH // 2)

    t_up_t = go.start(tok_hbm.at[top], tx.at[0, top], dx=1)
    t_dn_l = go.start(tok_hbm.at[low], tx.at[1, low], dx=3)
    w_up_t = go.start(wq.at[wtop], wy.at[y, wtop], dy=1)
    w_dn_l = go.start(wq.at[wlow], wy.at[y, wlow], dy=3)
    w_up_l = go.start(wq.at[wlow], wy.at[y, wlow], dy=1)
    w_dn_t = go.start(wq.at[wtop], wy.at[y, wtop], dy=3)

    def pair_part(half, into):
        rows = tok[pl.ds(pl.multiple_of(half * HALF, HALF), HALF), :]
        for g in range(4):
            part = jnp.dot(rows, wkv[:, pl.ds(g * 256, 256)], preferred_element_type=F32)
            for i in range(2):
                h = 2 * g + i
                into[h % 4, :, pl.ds((h // 4) * HEAD, HEAD)] = part[:, i * HEAD : (i + 1) * HEAD].astype(into.dtype)

    loads[0].wait()
    loads[1].wait()
    pair_part(1 - c, kv_sib_s)
    sib = go.start(kv_sib_s, kv_sib_r, dc=1)
    pair_part(c, kv_mine)
    sib.wait_recv()
    kv_z = []
    for r in (2, 1, 3):
        d = (z + r) % 4
        kv_z_s[r - 1] = (kv_mine[d] + kv_sib_r[d].astype(F32)).astype(BF16)
        kv_z.append(go.start(kv_z_s.at[r - 1], kv_z_r.at[r - 1], dz=r))
    loads[2].wait()
    loads[3].wait()
    for copy in kv_z:
        copy.wait_recv()
    own_pair = kv_mine[z] + kv_sib_r[z].astype(F32)
    for r in range(3):
        own_pair = own_pair + kv_z_r[r].astype(F32)
    for i in range(2):
        part = own_pair[i * BLK : (i + 1) * BLK]
        kv[32 * c + 2 * s + i, :, pl.ds(0, HEAD)] = turn(part[:, :HEAD], order[4 * s + 2 * c + i], table).astype(BF16)
        kv[32 * c + 2 * s + i, :, pl.ds(HEAD, HEAD)] = part[:, HEAD:].T.astype(BF16)

    def blocks(dy, column, n):
        return kv.at[pl.ds(32 * c + 8 * ((y + dy) % 4) + 2 * column, 2 * n)]

    own = blocks(0, x, 1)
    kv_x = {r: go.start(own, own, dx=r) for r in (1, 3, 2)}

    def kv_along_y(r):
        piece = blocks(0, (x + 4 - r) % 4, 1)
        return go.start(piece, piece, dy=1), go.start(piece, piece, dy=3)

    kv_y = {0: kv_along_y(0)}
    t_up_l = go.start(tok_hbm.at[low], tx.at[0, low], dx=1)
    t_dn_t = go.start(tok_hbm.at[top], tx.at[1, top], dx=3)

    w_up_t.wait_recv()
    piece = wy.at[(y + 3) % 4, wtop]
    w_rel_up = go.start(piece, piece, dy=1)
    w_dn_l.wait_recv()
    piece = wy.at[(y + 1) % 4, wlow]
    w_rel_dn = go.start(piece, piece, dy=3)
    w_up_l.wait_recv()
    w_dn_t.wait_recv()

    def project(u, rows_ref):
        def one(g, carry):
            part = jnp.dot(rows_ref[...], wy[g], preferred_element_type=F32)
            first, second = part[:, :HEAD], part[:, HEAD:]
            q_mine[u, g] = jnp.where(c == 0, first, second)
            q_sib_s[u, g] = jnp.where(c == 0, second, first).astype(BF16)
            return carry

        lax.fori_loop(0, 4, one, 0)
        return go.start(q_sib_s.at[u], q_sib_r.at[u], dc=1)

    def spread(u, copy):
        copy.wait_recv()
        sent = []
        for r in (2, 1, 3):
            d = (z + r) % 4
            q_z_s[u, r - 1] = (q_mine[u, d] + q_sib_r[u, d].astype(F32)).astype(BF16)
            sent.append(go.start(q_z_s.at[u, r - 1], q_z_r.at[u, r - 1], dz=r))
        return sent

    scale = math.log2(math.e) / math.sqrt(HEAD)

    def spot_of(u, i):
        t, h = UNITS[u]
        return 4 * (4 * y + (x + SHIFT[t]) % 4) + 2 * h + i

    def block_at(u, i):
        return order[spot_of(u, i)]

    def finish(u, sent):
        for copy in sent:
            copy.wait_recv()
        for i in range(2):
            rows = pl.ds(i * BLK, BLK)
            total = q_mine[u, z, rows, :] + q_sib_r[u, z, rows, :].astype(F32)
            for r in range(3):
                total = total + q_z_r[u, r, rows, :].astype(F32)
            q[u, rows, :] = (turn(total, block_at(u, i), table) * scale).astype(BF16)

    def attend(units):
        for k, (u, i) in enumerate([(u, i) for u in units for i in range(2)]):
            block = block_at(u, i)
            query = q[u, pl.ds(i * BLK, BLK), :]
            pos = lax.broadcasted_iota(jnp.int32, (1, BLK), 1) + block * BLK
            begin = jnp.zeros((1, BLK), jnp.int32)
            end = jnp.int32(0)
            for d in range(16):
                end = end + lengths[d]
                begin = jnp.where(pos >= end, end, begin)
            row = lax.broadcasted_iota(jnp.int32, (BLK, BLK), 0)
            ahead = row - (begin - (block - (WINDOW_BLOCKS - 1)) * BLK)
            causal = row <= lax.broadcasted_iota(jnp.int32, (BLK, BLK), 1)
            largest = jnp.full((BLK, BLK), NEG, F32)
            held = [where[WINDOW_BLOCKS * spot_of(u, i) + j] for j in range(WINDOW_BLOCKS)]
            keys = jnp.concatenate([kv[n, :, pl.ds(0, HEAD)] for n in held], axis=0)
            score[k] = lax.dot_general(keys, query, (((1,), (1,)), ((), ())), preferred_element_type=F32)
            for j in range(WINDOW_BLOCKS):
                allowed = ahead >= -j * BLK
                if j == WINDOW_BLOCKS - 1:
                    allowed = allowed & causal
                v = jnp.where(allowed, score[k, pl.ds(j * BLK, BLK), :], NEG)
                score[k, pl.ds(j * BLK, BLK), :] = v
                largest = jnp.maximum(largest, v)
            largest = jnp.max(largest, axis=0, keepdims=True)
            total = jnp.zeros((BLK, BLK), F32)
            parts = []
            for j in range(WINDOW_BLOCKS):
                w = jnp.exp2(score[k, pl.ds(j * BLK, BLK), :] - largest)
                total = total + w
                parts.append(w.astype(BF16))
            weights = jnp.concatenate(parts, axis=0)
            values = jnp.concatenate([kv[n, :, pl.ds(HEAD, HEAD)] for n in held], axis=1)
            mixed = jnp.dot(values, weights, preferred_element_type=F32)
            mixed = (mixed / jnp.sum(total, axis=0, keepdims=True)).T.astype(BF16)
            t, h = UNITS[u]
            if t == 0:
                att[z, c, x, pl.ds(h * HALF + i * BLK, BLK), :] = mixed
            else:
                away[u - 2, pl.ds(i * BLK, BLK), :] = mixed

    home, lifts, relays = {}, {}, {}

    def source(t):
        return (x + 4 - SHIFT[t]) % 4

    def part_of(u):
        return pl.ds(UNITS[u][1] * HALF, HALF)

    def hop(u):
        home[u] = go.start(away.at[u - 2], att.at[z, c, x, part_of(u)], dx=SHIFT[UNITS[u][0]])

    def lift(u):
        if u in home:
            home[u].wait_recv()
        piece = att.at[z, c, source(UNITS[u][0]), part_of(u)]
        lifts[u] = go.start(piece, piece, dz=1), go.start(piece, piece, dz=3)

    def relay(u):
        t, h = UNITS[u]
        lifts[u][h].wait_recv()
        piece = att.at[(z + (1 if h else 3)) % 4, c, source(t), part_of(u)]
        relays[u] = go.start(piece, piece, dz=3 if h else 1)

    shared = {}

    def share(r, t):
        piece = att.at[(z + r) % 4, c, source(t)]
        shared[r, t] = go.start(piece, piece, dc=1)

    def units_of(t):
        return [u for u in range(8) if UNITS[u][0] == t]

    def settle(t):
        for u in units_of(t):
            lifts[u][1 - UNITS[u][1]].wait_recv()
        share(3, t)
        share(1, t)
        for u in units_of(t):
            relays[u].wait_recv()
        share(2, t)

    def product(pieces, cols):
        left = jnp.concatenate([att[d, k, source(t)] for d, t in pieces for k in range(2)], axis=1)
        right = jnp.concatenate(
            [wo[pl.ds(pl.multiple_of((4 * d + source(t)) * 256, 256), 256), cols] for d, t in pieces], axis=0
        )
        return jnp.dot(left, right, preferred_element_type=F32)

    def multiply(pieces, first):
        def tile(n, carry):
            cols = pl.ds(pl.multiple_of(n * 256, 256), 256)
            part = product(pieces, cols)
            acc[:, cols] = part if first else acc[:, cols] + part
            return carry

        lax.fori_loop(0, 4, tile, 0)

    def bring(r, ts):
        for t in ts:
            shared[r, t].wait_recv()

    row = lambda r: blocks(r, 0, 4)
    kv_sib, kv_rel = [], []

    w_rel_up.wait_recv()
    w_rel_dn.wait_recv()
    sib0 = project(0, tok.at[top])
    sib1 = project(1, tok.at[low])
    sent0 = spread(0, sib0)
    for r in (1, 3):
        kv_x[r].wait_recv()
        kv_y[r] = kv_along_y(r)
    sent1 = spread(1, sib1)
    t_up_t.wait_recv()
    sib2 = project(2, tx.at[0, top])
    t_dn_l.wait_recv()
    sib3 = project(3, tx.at[1, low])
    kv_x[2].wait_recv()
    kv_y[2] = kv_along_y(2)
    kv_sib.append(go.start(row(0), row(0), dc=1))
    t_rel_up = go.start(tx.at[0, top], tx.at[2, top], dx=1)
    t_rel_dn = go.start(tx.at[1, low], tx.at[2, low], dx=3)
    sent2 = spread(2, sib2)
    sent3 = spread(3, sib3)
    finish(0, sent0)
    finish(1, sent1)

    def kv_pass(r):
        up = r % 2 == 0
        kv_y[r][0 if up else 1].wait_recv()
        piece = blocks(3 if up else 1, (x + 4 - r) % 4, 1)
        kv_rel.append(go.start(piece, piece, dy=1 if up else 3))

    kv_pass(0)
    kv_pass(1)
    t_up_l.wait_recv()
    sib4 = project(4, tx.at[0, low])
    t_dn_t.wait_recv()
    sib5 = project(5, tx.at[1, top])
    finish(2, sent2)
    finish(3, sent3)
    kv_pass(3)
    kv_pass(2)
    sent4 = spread(4, sib4)
    sent5 = spread(5, sib5)
    for r in range(4):
        kv_y[r][1 if r % 2 == 0 else 0].wait_recv()
    kv_sib.append(go.start(row(3), row(3), dc=1))
    kv_sib.append(go.start(row(1), row(1), dc=1))
    for copy in kv_rel:
        copy.wait_recv()
    kv_sib.append(go.start(row(2), row(2), dc=1))
    for copy in kv_sib:
        copy.wait_recv()
    attend((0, 1))
    lift(0)
    lift(1)
    share(0, 0)
    t_rel_up.wait_recv()
    sib6 = project(6, tx.at[2, top])
    t_rel_dn.wait_recv()
    sib7 = project(7, tx.at[2, low])
    attend((2, 3))
    hop(2)
    hop(3)
    sent6 = spread(6, sib6)
    sent7 = spread(7, sib7)
    finish(4, sent4)
    finish(5, sent5)
    relay(0)
    relay(1)
    attend((4, 5))
    hop(4)
    hop(5)
    lift(2)
    lift(3)
    finish(6, sent6)
    finish(7, sent7)
    attend((6, 7))
    hop(6)
    hop(7)
    lift(4)
    lift(5)
    share(0, 1)
    share(0, 2)
    relay(2)
    relay(3)
    settle(0)
    loads[4].wait()
    bring(0, (0, 1, 2))
    multiply([(z, 0), (z, 1), (z, 2)], True)
    lift(6)
    lift(7)
    share(0, 3)
    relay(4)
    relay(5)
    settle(1)
    settle(2)
    for r in (1, 3, 2):
        bring(r, (0, 1, 2))
        d = (z + r) % 4
        multiply([(d, 0), (d, 1), (d, 2)], False)
        if r == 1:
            relay(6)
            relay(7)
    settle(3)
    for r in range(4):
        bring(r, (3,))
    last = [(d, 3) for d in range(4)]

    def close(n, carry):
        cols = pl.ds(pl.multiple_of(n * 256, 256), 256)
        out[:, cols] = (acc[:, cols] + product(last, cols)).astype(BF16)
        return carry

    lax.fori_loop(0, 4, close, 0)
    go.drain()


def layer(order, where, lengths, tok, wq, wkv, wo):
    vm = pl.BlockSpec(memory_space=pltpu.VMEM)
    sm = pl.BlockSpec(memory_space=pltpu.SMEM)
    hbm = pl.BlockSpec(memory_space=pl.ANY)
    n = 128
    return pl.pallas_call(
        layer_kernel,
        out_shape=jax.ShapeDtypeStruct((ROWS, WIDTH), BF16),
        in_specs=[sm] * 3 + [hbm] * 5,
        out_specs=vm,
        scratch_shapes=[
            pltpu.VMEM((3 * BLK, HEAD), F32),
            pltpu.VMEM((ROWS, WIDTH), BF16),
            pltpu.VMEM((WIDTH, WIDTH), BF16),
            pltpu.VMEM((4 * WIDTH, WIDTH), BF16),
            pltpu.VMEM((3, ROWS, WIDTH), BF16),
            pltpu.VMEM((4, WIDTH, 256), BF16),
            pltpu.VMEM((64, BLK, 256), BF16),
            pltpu.VMEM((4, 256, 256), F32),
            pltpu.VMEM((4, 256, 256), BF16),
            pltpu.VMEM((4, 256, 256), BF16),
            pltpu.VMEM((3, 256, 256), BF16),
            pltpu.VMEM((3, 256, 256), BF16),
            pltpu.VMEM((8, 4, HALF, HEAD), F32),
            pltpu.VMEM((8, 4, HALF, HEAD), BF16),
            pltpu.VMEM((8, 4, HALF, HEAD), BF16),
            pltpu.VMEM((8, 3, HALF, HEAD), BF16),
            pltpu.VMEM((8, 3, HALF, HEAD), BF16),
            pltpu.VMEM((8, HALF, HEAD), BF16),
            pltpu.VMEM((4, WINDOW_BLOCKS * BLK, BLK), F32),
            pltpu.VMEM((6, HALF, HEAD), BF16),
            pltpu.VMEM((4, 2, 4, ROWS, HEAD), BF16),
            pltpu.VMEM((ROWS, WIDTH), F32),
            pltpu.SemaphoreType.DMA((5,)),
            pltpu.SemaphoreType.DMA((n,)),
            pltpu.SemaphoreType.DMA((n,)),
        ],
        compiler_params=pltpu.CompilerParams(
            collective_id=0, has_side_effects=True, vmem_limit_bytes=60 << 20
        ),
    )(order, where, lengths, jnp.asarray(rope_tables()), tok, wq, wkv, wo)


def body(tokens, query_weight, key_value_matrix, output_weight, document_lengths, block_order):
    held = np.arange(64, dtype=np.int32)
    slot = held % 4 // 2 * 32 + held // 4 * 2 + held % 2
    wanted = jnp.maximum(block_order[:, None] + np.arange(1 - WINDOW_BLOCKS, 1, dtype=np.int32), 0)
    match = block_order[:, None] == wanted.reshape(1, -1)
    where = jnp.sum(jnp.where(match, slot[:, None], 0), axis=0)
    return layer(
        block_order, where, document_lengths, tokens, query_weight, key_value_matrix, output_weight
    )


def solution(mesh):
    placed = (P("seq", "mp"), P("mp", "seq"), P("mp", None), P(None, "mp"), P(), P())
    return jax.shard_map(
        body, mesh=mesh, in_specs=placed, out_specs=P("seq", "mp"), check_vma=False
    )
```

```python
import functools
import math

import jax
import jax.numpy as jnp
import numpy as np
from jax import lax
from jax.experimental import pallas as pl
from jax.experimental.pallas import tpu as pltpu
from jax.sharding import PartitionSpec as P

MESH = pl.DeviceIdType.MESH
HEAD = 128
BLK = 128
ROWS = 512
WIDTH = 1024
WINDOW_BLOCKS = 17
ROPE_BASE = 500000.0
NEG = -1e30
BF16 = jnp.bfloat16
F32 = jnp.float32


UNITS = ((0, 0), (0, 1), (1, 0), (2, 1), (1, 1), (2, 0), (3, 0), (3, 1))
SHIFT = (0, 3, 1, 2)
HALF = ROWS // 2


def rope_tables():
    half = HEAD // 2
    inverse = np.exp(-(2.0 * np.arange(half) / HEAD) * np.log(ROPE_BASE))
    within = np.arange(BLK)[:, None] * inverse[None, :]
    start = (np.arange(64) * BLK)[:, None] * inverse[None, :]

    def both(values, sign):
        return np.concatenate([sign * values, values], axis=1).astype(np.float32)

    return np.concatenate(
        [
            both(np.cos(within), 1.0),
            both(np.sin(within), -1.0),
            both(np.cos(start), 1.0),
            both(np.sin(start), -1.0),
        ]
    )


def place():
    s = lax.axis_index("seq")
    m = lax.axis_index("mp")
    return s // 4, s % 4, m // 2, m % 2


def at(y, x, z, c, dy=0, dx=0, dz=0, dc=0):
    return (((y + dy) % 4) * 4 + (x + dx) % 4, ((z + dz) % 4) * 2 + (c + dc) % 2)


def greet(here, offsets):
    barrier = pltpu.get_barrier_semaphore()
    for off in offsets:
        pl.semaphore_signal(barrier, inc=1, device_id=at(*here, **off), device_id_type=MESH)
    pl.semaphore_wait(barrier, len(offsets))


class Copies:
    def __init__(self, here, send, recv):
        self.here, self.send, self.recv = here, send, recv
        self.count, self.open = 0, []

    def start(self, src, dst, **off):
        k = self.count
        self.count += 1
        copy = pltpu.make_async_remote_copy(
            src_ref=src,
            dst_ref=dst,
            send_sem=self.send.at[k],
            recv_sem=self.recv.at[k],
            device_id=at(*self.here, **off),
            device_id_type=MESH,
        )
        copy.start()
        self.open.append(copy)
        return copy

    def drain(self):
        for copy in self.open:
            copy.wait_send()


def turn(values, block, table):
    cr, sr = table[pl.ds(0, BLK), :], table[pl.ds(BLK, BLK), :]
    c0 = table[pl.ds(2 * BLK + block, 1), :]
    s0 = table[pl.ds(2 * BLK + 64 + block, 1), :]
    cosine = c0 * cr - s0 * sr
    sine = s0 * cr + c0 * sr
    return values * cosine + pltpu.roll(values, HEAD // 2, 1) * sine


OFFSETS = [
    dict(dx=1),
    dict(dx=3),
    dict(dx=2),
    dict(dy=1),
    dict(dy=3),
    dict(dz=1),
    dict(dz=3),
    dict(dz=2),
    dict(dc=1),
]


def layer_kernel(
    order, lengths, table_hbm, tok_hbm, wq, wkv_hbm, wo_hbm, out,
    table, tok, wkv, wo, tx, wy, kv, kv_mine, kv_sib_s, kv_sib_r, kv_z_s, kv_z_r,
    q_mine, q_sib_s, q_sib_r, q_z_s, q_z_r, q, score, away, att, acc, windows, where, local, send, recv,
):
    here = place()
    y, x, z, c = here
    s = 4 * y + x
    loads = [
        pltpu.make_async_copy(src, dst, local.at[k])
        for k, (src, dst) in enumerate(
            ((tok_hbm, tok), (wkv_hbm, wkv), (table_hbm, table), (wq, wy.at[y]), (wo_hbm, wo))
        )
    ]
    for load in loads[:4]:
        load.start()
    greet(here, OFFSETS)
    go = Copies(here, send, recv)
    top, low = pl.ds(0, HALF), pl.ds(HALF, HALF)
    wtop, wlow = pl.ds(0, WIDTH // 2), pl.ds(WIDTH // 2, WIDTH // 2)

    t_up_t = go.start(tok_hbm.at[top], tx.at[0, top], dx=1)
    t_dn_l = go.start(tok_hbm.at[low], tx.at[1, low], dx=3)
    w_up_t = go.start(wq.at[wtop], wy.at[y, wtop], dy=1)
    w_dn_l = go.start(wq.at[wlow], wy.at[y, wlow], dy=3)
    w_up_l = go.start(wq.at[wlow], wy.at[y, wlow], dy=1)
    w_dn_t = go.start(wq.at[wtop], wy.at[y, wtop], dy=3)

    def pair_part(half, into):
        rows = tok[pl.ds(pl.multiple_of(half * HALF, HALF), HALF), :]
        for g in range(4):
            part = jnp.dot(rows, wkv[:, pl.ds(g * 256, 256)], preferred_element_type=F32)
            for i in range(2):
                h = 2 * g + i
                into[h % 4, :, pl.ds((h // 4) * HEAD, HEAD)] = part[:, i * HEAD : (i + 1) * HEAD].astype(into.dtype)

    loads[0].wait()
    loads[1].wait()
    pair_part(1 - c, kv_sib_s)
    sib = go.start(kv_sib_s, kv_sib_r, dc=1)
    pair_part(c, kv_mine)
    sib.wait_recv()
    kv_z = []
    for r in (2, 1, 3):
        d = (z + r) % 4
        kv_z_s[r - 1] = (kv_mine[d] + kv_sib_r[d].astype(F32)).astype(BF16)
        kv_z.append(go.start(kv_z_s.at[r - 1], kv_z_r.at[r - 1], dz=r))
    loads[4].start()
    lane = lax.broadcasted_iota(jnp.int32, (16, BLK), 1)
    line = lax.broadcasted_iota(jnp.int32, (16, BLK), 0)
    wanted = lane - (WINDOW_BLOCKS - 1)
    for n in range(16):
        t, h = UNITS[n // 2]
        mine = order[4 * (4 * y + (x + SHIFT[t]) % 4) + 2 * h + n % 2]
        wanted = wanted + jnp.where(line == n, mine, 0)
    wanted = jnp.maximum(wanted, 0)
    found = jnp.zeros((16, BLK), jnp.int32)
    for n in range(64):
        found = jnp.where(wanted == order[n], n % 4 // 2 * 32 + n // 4 * 2 + n % 2, found)
    windows[...] = found
    table_copy = pltpu.make_async_copy(windows, where, local.at[5])
    table_copy.start()
    loads[2].wait()
    loads[3].wait()
    table_copy.wait()
    w_up_t.wait_recv()
    piece = wy.at[(y + 3) % 4, wtop]
    w_rel_up = go.start(piece, piece, dy=1)
    w_dn_l.wait_recv()
    piece = wy.at[(y + 1) % 4, wlow]
    w_rel_dn = go.start(piece, piece, dy=3)
    w_up_l.wait_recv()
    w_dn_t.wait_recv()
    for copy in kv_z:
        copy.wait_recv()
    own_pair = kv_mine[z] + kv_sib_r[z].astype(F32)
    for r in range(3):
        own_pair = own_pair + kv_z_r[r].astype(F32)
    for i in range(2):
        part = own_pair[i * BLK : (i + 1) * BLK]
        kv[32 * c + 2 * s + i, :, pl.ds(0, HEAD)] = turn(part[:, :HEAD], order[4 * s + 2 * c + i], table).astype(BF16)
        kv[32 * c + 2 * s + i, :, pl.ds(HEAD, HEAD)] = part[:, HEAD:].T.astype(BF16)

    def blocks(dy, column, n):
        return kv.at[pl.ds(32 * c + 8 * ((y + dy) % 4) + 2 * column, 2 * n)]

    own = blocks(0, x, 1)
    kv_x = {r: go.start(own, own, dx=r) for r in (1, 3, 2)}

    def kv_along_y(r):
        piece = blocks(0, (x + 4 - r) % 4, 1)
        return go.start(piece, piece, dy=1), go.start(piece, piece, dy=3)

    kv_y = {0: kv_along_y(0)}

    def project(u, rows_ref):
        def one(g, carry):
            part = jnp.dot(rows_ref[...], wy[g], preferred_element_type=F32)
            first, second = part[:, :HEAD], part[:, HEAD:]
            q_mine[u, g] = jnp.where(c == 0, first, second)
            q_sib_s[u, g] = jnp.where(c == 0, second, first).astype(BF16)
            return carry

        lax.fori_loop(0, 4, one, 0)
        return go.start(q_sib_s.at[u], q_sib_r.at[u], dc=1)

    def spread(u, copy):
        copy.wait_recv()
        sent = []
        for r in (2, 1, 3):
            d = (z + r) % 4
            q_z_s[u, r - 1] = (q_mine[u, d] + q_sib_r[u, d].astype(F32)).astype(BF16)
            sent.append(go.start(q_z_s.at[u, r - 1], q_z_r.at[u, r - 1], dz=r))
        return sent

    scale = math.log2(math.e) / math.sqrt(HEAD)

    def spot_of(u, i):
        t, h = UNITS[u]
        return 4 * (4 * y + (x + SHIFT[t]) % 4) + 2 * h + i

    def block_at(u, i):
        return order[spot_of(u, i)]

    def finish(u, sent):
        for copy in sent:
            copy.wait_recv()
        for i in range(2):
            rows = pl.ds(i * BLK, BLK)
            total = q_mine[u, z, rows, :] + q_sib_r[u, z, rows, :].astype(F32)
            for r in range(3):
                total = total + q_z_r[u, r, rows, :].astype(F32)
            q[u, rows, :] = (turn(total, block_at(u, i), table) * scale).astype(BF16)

    def attend(units):
        for k, (u, i) in enumerate([(u, i) for u in units for i in range(2)]):
            block = block_at(u, i)
            query = q[u, pl.ds(i * BLK, BLK), :]
            pos = lax.broadcasted_iota(jnp.int32, (1, BLK), 1) + block * BLK
            begin = jnp.zeros((1, BLK), jnp.int32)
            end = jnp.int32(0)
            for d in range(16):
                end = end + lengths[d]
                begin = jnp.where(pos >= end, end, begin)
            row = lax.broadcasted_iota(jnp.int32, (BLK, BLK), 0)
            ahead = row - (begin - (block - (WINDOW_BLOCKS - 1)) * BLK)
            causal = row <= lax.broadcasted_iota(jnp.int32, (BLK, BLK), 1)
            largest = jnp.full((BLK, BLK), NEG, F32)
            held = [where[2 * u + i, j] for j in range(WINDOW_BLOCKS)]
            keys = jnp.concatenate([kv[n, :, pl.ds(0, HEAD)] for n in held], axis=0)
            score[k] = lax.dot_general(keys, query, (((1,), (1,)), ((), ())), preferred_element_type=F32)
            for j in range(WINDOW_BLOCKS):
                allowed = ahead >= -j * BLK
                if j == WINDOW_BLOCKS - 1:
                    allowed = allowed & causal
                v = jnp.where(allowed, score[k, pl.ds(j * BLK, BLK), :], NEG)
                score[k, pl.ds(j * BLK, BLK), :] = v
                largest = jnp.maximum(largest, v)
            largest = jnp.max(largest, axis=0, keepdims=True)
            total = jnp.zeros((BLK, BLK), F32)
            parts = []
            for j in range(WINDOW_BLOCKS):
                w = jnp.exp2(score[k, pl.ds(j * BLK, BLK), :] - largest)
                total = total + w
                parts.append(w.astype(BF16))
            weights = jnp.concatenate(parts, axis=0)
            values = jnp.concatenate([kv[n, :, pl.ds(HEAD, HEAD)] for n in held], axis=1)
            mixed = jnp.dot(values, weights, preferred_element_type=F32)
            mixed = (mixed / jnp.sum(total, axis=0, keepdims=True)).T.astype(BF16)
            t, h = UNITS[u]
            if t == 0:
                att[z, c, x, pl.ds(h * HALF + i * BLK, BLK), :] = mixed
            else:
                away[u - 2, pl.ds(i * BLK, BLK), :] = mixed

    home, lifts, relays = {}, {}, {}

    def source(t):
        return (x + 4 - SHIFT[t]) % 4

    def part_of(u):
        return pl.ds(UNITS[u][1] * HALF, HALF)

    def hop(u):
        home[u] = go.start(away.at[u - 2], att.at[z, c, x, part_of(u)], dx=SHIFT[UNITS[u][0]])

    def lift(u):
        if u in home:
            home[u].wait_recv()
        piece = att.at[z, c, source(UNITS[u][0]), part_of(u)]
        lifts[u] = go.start(piece, piece, dz=1), go.start(piece, piece, dz=3)

    def relay(u):
        t, h = UNITS[u]
        lifts[u][h].wait_recv()
        piece = att.at[(z + (1 if h else 3)) % 4, c, source(t), part_of(u)]
        relays[u] = go.start(piece, piece, dz=3 if h else 1)

    shared = {}

    def share(r, t):
        piece = att.at[(z + r) % 4, c, source(t)]
        shared[r, t] = go.start(piece, piece, dc=1)

    def units_of(t):
        return [u for u in range(8) if UNITS[u][0] == t]

    def settle(t):
        for u in units_of(t):
            lifts[u][1 - UNITS[u][1]].wait_recv()
        share(3, t)
        share(1, t)
        for u in units_of(t):
            relays[u].wait_recv()
        share(2, t)

    def product(pieces, cols):
        left = jnp.concatenate([att[d, k, source(t)] for d, t in pieces for k in range(2)], axis=1)
        right = jnp.concatenate(
            [wo[pl.ds(pl.multiple_of((4 * d + source(t)) * 256, 256), 256), cols] for d, t in pieces], axis=0
        )
        return jnp.dot(left, right, preferred_element_type=F32)

    def multiply(pieces, first):
        def tile(n, carry):
            cols = pl.ds(pl.multiple_of(n * 256, 256), 256)
            part = product(pieces, cols)
            acc[:, cols] = part if first else acc[:, cols] + part
            return carry

        lax.fori_loop(0, 4, tile, 0, unroll=2)

    def bring(r, ts):
        for t in ts:
            shared[r, t].wait_recv()

    row = lambda r: blocks(r, 0, 4)
    kv_sib, kv_rel = [], []

    def kv_pass(r):
        up = r % 2 == 0
        kv_y[r][0 if up else 1].wait_recv()
        piece = blocks(3 if up else 1, (x + 4 - r) % 4, 1)
        kv_rel.append(go.start(piece, piece, dy=1 if up else 3))

    w_rel_up.wait_recv()
    w_rel_dn.wait_recv()
    sib0 = project(0, tok.at[top])
    for r in (1, 3):
        kv_x[r].wait_recv()
        kv_y[r] = kv_along_y(r)
    t_up_l = go.start(tok_hbm.at[low], tx.at[0, low], dx=1)
    t_dn_t = go.start(tok_hbm.at[top], tx.at[1, top], dx=3)
    kv_x[2].wait_recv()
    kv_y[2] = kv_along_y(2)
    kv_sib.append(go.start(row(0), row(0), dc=1))
    sib1 = project(1, tok.at[low])
    spread0 = spread(0, sib0)
    kv_pass(0)
    kv_pass(1)
    t_up_t.wait_recv()
    sib2 = project(2, tx.at[0, top])
    spread1 = spread(1, sib1)
    t_dn_l.wait_recv()
    t_rel_up = go.start(tx.at[0, top], tx.at[2, top], dx=1)
    t_rel_dn = go.start(tx.at[1, low], tx.at[2, low], dx=3)
    sib3 = project(3, tx.at[1, low])
    spread2 = spread(2, sib2)
    kv_pass(3)
    spread3 = spread(3, sib3)
    kv_pass(2)
    finish(0, spread0)
    finish(1, spread1)
    for r in range(4):
        kv_y[r][1 if r % 2 == 0 else 0].wait_recv()
    kv_sib.append(go.start(row(3), row(3), dc=1))
    kv_sib.append(go.start(row(1), row(1), dc=1))
    finish(2, spread2)
    finish(3, spread3)
    for copy in kv_rel:
        copy.wait_recv()
    kv_sib.append(go.start(row(2), row(2), dc=1))
    for copy in kv_sib:
        copy.wait_recv()
    attend((0, 1))
    lift(0)
    lift(1)
    share(0, 0)
    t_up_l.wait_recv()
    sib4 = project(4, tx.at[0, low])
    t_dn_t.wait_recv()
    sib5 = project(5, tx.at[1, top])
    attend((2, 3))
    hop(2)
    hop(3)
    spread4 = spread(4, sib4)
    spread5 = spread(5, sib5)
    relay(0)
    relay(1)
    t_rel_up.wait_recv()
    sib6 = project(6, tx.at[2, top])
    lift(2)
    lift(3)
    t_rel_dn.wait_recv()
    sib7 = project(7, tx.at[2, low])
    spread6 = spread(6, sib6)
    finish(4, spread4)
    finish(5, spread5)
    spread7 = spread(7, sib7)
    attend((4, 5))
    hop(4)
    hop(5)
    relay(2)
    relay(3)
    settle(0)
    lift(4)
    lift(5)
    share(0, 1)
    share(0, 2)
    loads[4].wait()
    for r in range(4):
        bring(r, (0,))
    multiply([(d, 0) for d in range(4)], True)
    finish(6, spread6)
    finish(7, spread7)
    attend((6, 7))
    hop(6)
    hop(7)
    relay(4)
    relay(5)
    lift(6)
    lift(7)
    share(0, 3)
    settle(1)
    for r in range(4):
        bring(r, (1,))
    multiply([(d, 1) for d in range(4)], False)
    settle(2)
    for r in range(4):
        bring(r, (2,))
    relay(6)
    relay(7)
    multiply([(d, 2) for d in range(4)], False)
    settle(3)
    for r in range(4):
        bring(r, (3,))
    last = [(d, 3) for d in range(4)]

    def close(n, carry):
        cols = pl.ds(pl.multiple_of(n * 256, 256), 256)
        out[:, cols] = (acc[:, cols] + product(last, cols)).astype(BF16)
        return carry

    lax.fori_loop(0, 4, close, 0)
    go.drain()


def layer(order, lengths, tok, wq, wkv, wo):
    vm = pl.BlockSpec(memory_space=pltpu.VMEM)
    sm = pl.BlockSpec(memory_space=pltpu.SMEM)
    hbm = pl.BlockSpec(memory_space=pl.ANY)
    n = 128
    return pl.pallas_call(
        layer_kernel,
        out_shape=jax.ShapeDtypeStruct((ROWS, WIDTH), BF16),
        in_specs=[sm] * 2 + [hbm] * 5,
        out_specs=vm,
        scratch_shapes=[
            pltpu.VMEM((3 * BLK, HEAD), F32),
            pltpu.VMEM((ROWS, WIDTH), BF16),
            pltpu.VMEM((WIDTH, WIDTH), BF16),
            pltpu.VMEM((4 * WIDTH, WIDTH), BF16),
            pltpu.VMEM((3, ROWS, WIDTH), BF16),
            pltpu.VMEM((4, WIDTH, 256), BF16),
            pltpu.VMEM((64, BLK, 256), BF16),
            pltpu.VMEM((4, 256, 256), F32),
            pltpu.VMEM((4, 256, 256), BF16),
            pltpu.VMEM((4, 256, 256), BF16),
            pltpu.VMEM((3, 256, 256), BF16),
            pltpu.VMEM((3, 256, 256), BF16),
            pltpu.VMEM((8, 4, HALF, HEAD), F32),
            pltpu.VMEM((8, 4, HALF, HEAD), BF16),
            pltpu.VMEM((8, 4, HALF, HEAD), BF16),
            pltpu.VMEM((8, 3, HALF, HEAD), BF16),
            pltpu.VMEM((8, 3, HALF, HEAD), BF16),
            pltpu.VMEM((8, HALF, HEAD), BF16),
            pltpu.VMEM((4, WINDOW_BLOCKS * BLK, BLK), F32),
            pltpu.VMEM((6, HALF, HEAD), BF16),
            pltpu.VMEM((4, 2, 4, ROWS, HEAD), BF16),
            pltpu.VMEM((ROWS, WIDTH), F32),
            pltpu.VMEM((16, BLK), jnp.int32),
            pltpu.SMEM((16, BLK), jnp.int32),
            pltpu.SemaphoreType.DMA((6,)),
            pltpu.SemaphoreType.DMA((n,)),
            pltpu.SemaphoreType.DMA((n,)),
        ],
        compiler_params=pltpu.CompilerParams(
            collective_id=0, has_side_effects=True, vmem_limit_bytes=54 << 20
        ),
    )(order, lengths, jnp.asarray(rope_tables()), tok, wq, wkv, wo)


def body(tokens, query_weight, key_value_matrix, output_weight, document_lengths, block_order):
    return layer(
        block_order, document_lengths, tokens, query_weight, key_value_matrix, output_weight
    )


def solution(mesh):
    placed = (P("seq", "mp"), P("mp", "seq"), P("mp", None), P(None, "mp"), P(), P())
    return jax.shard_map(
        body, mesh=mesh, in_specs=placed, out_specs=P("seq", "mp"), check_vma=False
    )
```

```python
import functools
import math

import jax
import jax.numpy as jnp
import numpy as np
from jax import lax
from jax.experimental import pallas as pl
from jax.experimental.pallas import tpu as pltpu
from jax.sharding import PartitionSpec as P

MESH = pl.DeviceIdType.MESH
HEAD = 128
BLK = 128
ROWS = 512
WIDTH = 1024
WINDOW_BLOCKS = 17
ROPE_BASE = 500000.0
NEG = -1e30
BF16 = jnp.bfloat16
F32 = jnp.float32


UNITS = ((0, 0), (0, 1), (1, 0), (2, 1), (1, 1), (2, 0), (3, 0), (3, 1))
SHIFT = (0, 3, 1, 2)
HALF = ROWS // 2


def rope_tables():
    half = HEAD // 2
    inverse = np.exp(-(2.0 * np.arange(half) / HEAD) * np.log(ROPE_BASE))
    within = np.arange(BLK)[:, None] * inverse[None, :]
    start = (np.arange(64) * BLK)[:, None] * inverse[None, :]

    def both(values, sign):
        return np.concatenate([sign * values, values], axis=1).astype(np.float32)

    return np.concatenate(
        [
            both(np.cos(within), 1.0),
            both(np.sin(within), -1.0),
            both(np.cos(start), 1.0),
            both(np.sin(start), -1.0),
        ]
    )


def place():
    s = lax.axis_index("seq")
    m = lax.axis_index("mp")
    return s // 4, s % 4, m // 2, m % 2


def at(y, x, z, c, dy=0, dx=0, dz=0, dc=0):
    return (((y + dy) % 4) * 4 + (x + dx) % 4, ((z + dz) % 4) * 2 + (c + dc) % 2)


def greet(here, offsets):
    barrier = pltpu.get_barrier_semaphore()
    for off in offsets:
        pl.semaphore_signal(barrier, inc=1, device_id=at(*here, **off), device_id_type=MESH)
    pl.semaphore_wait(barrier, len(offsets))


class Copies:
    def __init__(self, here, send, recv):
        self.here, self.send, self.recv = here, send, recv
        self.count, self.open = 0, []

    def start(self, src, dst, **off):
        k = self.count
        self.count += 1
        copy = pltpu.make_async_remote_copy(
            src_ref=src,
            dst_ref=dst,
            send_sem=self.send.at[k],
            recv_sem=self.recv.at[k],
            device_id=at(*self.here, **off),
            device_id_type=MESH,
        )
        copy.start()
        self.open.append(copy)
        return copy

    def drain(self):
        for copy in self.open:
            copy.wait_send()


def turn(values, block, table):
    cr, sr = table[pl.ds(0, BLK), :], table[pl.ds(BLK, BLK), :]
    c0 = table[pl.ds(2 * BLK + block, 1), :]
    s0 = table[pl.ds(2 * BLK + 64 + block, 1), :]
    cosine = c0 * cr - s0 * sr
    sine = s0 * cr + c0 * sr
    return values * cosine + pltpu.roll(values, HEAD // 2, 1) * sine


OFFSETS = [
    dict(dx=1),
    dict(dx=3),
    dict(dx=2),
    dict(dy=1),
    dict(dy=3),
    dict(dz=1),
    dict(dz=3),
    dict(dz=2),
    dict(dc=1),
]


def layer_kernel(
    order, lengths, table_hbm, tok_hbm, wq, wkv_hbm, wo_hbm, out,
    table, tok, wkv, wo, tx, wy, kv, kv_mine, kv_sib_s, kv_sib_r, kv_z_s, kv_z_r,
    q_mine, q_sib_s, q_sib_r, q_z_s, q_z_r, q, score, away, att, acc, windows, where, local, send, recv,
):
    here = place()
    y, x, z, c = here
    s = 4 * y + x
    loads = [
        pltpu.make_async_copy(src, dst, local.at[k])
        for k, (src, dst) in enumerate(
            ((tok_hbm, tok), (wkv_hbm, wkv), (table_hbm, table), (wq, wy.at[y]), (wo_hbm, wo))
        )
    ]
    for load in loads[:4]:
        load.start()
    greet(here, OFFSETS)
    go = Copies(here, send, recv)
    top, low = pl.ds(0, HALF), pl.ds(HALF, HALF)
    wtop, wlow = pl.ds(0, WIDTH // 2), pl.ds(WIDTH // 2, WIDTH // 2)

    t_up_t = go.start(tok_hbm.at[top], tx.at[0, top], dx=1)
    t_dn_l = go.start(tok_hbm.at[low], tx.at[1, low], dx=3)
    w_up_t = go.start(wq.at[wtop], wy.at[y, wtop], dy=1)
    w_dn_l = go.start(wq.at[wlow], wy.at[y, wlow], dy=3)
    w_up_l = go.start(wq.at[wlow], wy.at[y, wlow], dy=1)
    w_dn_t = go.start(wq.at[wtop], wy.at[y, wtop], dy=3)

    def pair_part(half, into):
        rows = tok[pl.ds(pl.multiple_of(half * HALF, HALF), HALF), :]
        for g in range(4):
            part = jnp.dot(rows, wkv[:, pl.ds(g * 256, 256)], preferred_element_type=F32)
            for i in range(2):
                h = 2 * g + i
                into[h % 4, :, pl.ds((h // 4) * HEAD, HEAD)] = part[:, i * HEAD : (i + 1) * HEAD].astype(into.dtype)

    loads[0].wait()
    loads[1].wait()
    pair_part(1 - c, kv_sib_s)
    sib = go.start(kv_sib_s, kv_sib_r, dc=1)
    pair_part(c, kv_mine)
    sib.wait_recv()
    kv_z = []
    for r in (2, 1, 3):
        d = (z + r) % 4
        kv_z_s[r - 1] = (kv_mine[d] + kv_sib_r[d].astype(F32)).astype(BF16)
        kv_z.append(go.start(kv_z_s.at[r - 1], kv_z_r.at[r - 1], dz=r))
    loads[4].start()
    lane = lax.broadcasted_iota(jnp.int32, (16, BLK), 1)
    line = lax.broadcasted_iota(jnp.int32, (16, BLK), 0)
    wanted = lane - (WINDOW_BLOCKS - 1)
    for n in range(16):
        t, h = UNITS[n // 2]
        mine = order[4 * (4 * y + (x + SHIFT[t]) % 4) + 2 * h + n % 2]
        wanted = wanted + jnp.where(line == n, mine, 0)
    wanted = jnp.maximum(wanted, 0)
    found = jnp.zeros((16, BLK), jnp.int32)
    for n in range(64):
        found = jnp.where(wanted == order[n], n % 4 // 2 * 32 + n // 4 * 2 + n % 2, found)
    windows[...] = found
    table_copy = pltpu.make_async_copy(windows, where, local.at[5])
    table_copy.start()
    loads[2].wait()
    loads[3].wait()
    table_copy.wait()
    w_up_t.wait_recv()
    piece = wy.at[(y + 3) % 4, wtop]
    w_rel_up = go.start(piece, piece, dy=1)
    w_dn_l.wait_recv()
    piece = wy.at[(y + 1) % 4, wlow]
    w_rel_dn = go.start(piece, piece, dy=3)
    w_up_l.wait_recv()
    w_dn_t.wait_recv()
    for copy in kv_z:
        copy.wait_recv()
    own_pair = kv_mine[z] + kv_sib_r[z].astype(F32)
    for r in range(3):
        own_pair = own_pair + kv_z_r[r].astype(F32)
    for i in range(2):
        part = own_pair[i * BLK : (i + 1) * BLK]
        kv[32 * c + 2 * s + i, :, pl.ds(0, HEAD)] = turn(part[:, :HEAD], order[4 * s + 2 * c + i], table).astype(BF16)
        kv[32 * c + 2 * s + i, :, pl.ds(HEAD, HEAD)] = part[:, HEAD:].T.astype(BF16)

    def blocks(dy, column, n):
        return kv.at[pl.ds(32 * c + 8 * ((y + dy) % 4) + 2 * column, 2 * n)]

    own = blocks(0, x, 1)
    kv_x = {r: go.start(own, own, dx=r) for r in (1, 3, 2)}

    def kv_along_y(r):
        piece = blocks(0, (x + 4 - r) % 4, 1)
        return go.start(piece, piece, dy=1), go.start(piece, piece, dy=3)

    kv_y = {0: kv_along_y(0)}

    def project(u, rows_ref):
        def one(g, carry):
            part = jnp.dot(rows_ref[...], wy[g], preferred_element_type=F32)
            first, second = part[:, :HEAD], part[:, HEAD:]
            q_mine[u, g] = jnp.where(c == 0, first, second)
            q_sib_s[u, g] = jnp.where(c == 0, second, first).astype(BF16)
            return carry

        lax.fori_loop(0, 4, one, 0, unroll=2)
        return go.start(q_sib_s.at[u], q_sib_r.at[u], dc=1)

    def spread(u, copy):
        copy.wait_recv()
        sent = []
        for r in (2, 1, 3):
            d = (z + r) % 4
            q_z_s[u, r - 1] = (q_mine[u, d] + q_sib_r[u, d].astype(F32)).astype(BF16)
            sent.append(go.start(q_z_s.at[u, r - 1], q_z_r.at[u, r - 1], dz=r))
        return sent

    scale = math.log2(math.e) / math.sqrt(HEAD)

    def spot_of(u, i):
        t, h = UNITS[u]
        return 4 * (4 * y + (x + SHIFT[t]) % 4) + 2 * h + i

    def block_at(u, i):
        return order[spot_of(u, i)]

    def finish(u, sent):
        for copy in sent:
            copy.wait_recv()
        for i in range(2):
            rows = pl.ds(i * BLK, BLK)
            total = q_mine[u, z, rows, :] + q_sib_r[u, z, rows, :].astype(F32)
            for r in range(3):
                total = total + q_z_r[u, r, rows, :].astype(F32)
            q[u, rows, :] = (turn(total, block_at(u, i), table) * scale).astype(BF16)

    def attend(units):
        for k, (u, i) in enumerate([(u, i) for u in units for i in range(2)]):
            block = block_at(u, i)
            query = q[u, pl.ds(i * BLK, BLK), :]
            pos = lax.broadcasted_iota(jnp.int32, (1, BLK), 1) + block * BLK
            begin = jnp.zeros((1, BLK), jnp.int32)
            end = jnp.int32(0)
            for d in range(16):
                end = end + lengths[d]
                begin = jnp.where(pos >= end, end, begin)
            row = lax.broadcasted_iota(jnp.int32, (BLK, BLK), 0)
            ahead = row - (begin - (block - (WINDOW_BLOCKS - 1)) * BLK)
            causal = row <= lax.broadcasted_iota(jnp.int32, (BLK, BLK), 1)
            largest = jnp.full((BLK, BLK), NEG, F32)
            held = [where[2 * u + i, j] for j in range(WINDOW_BLOCKS)]
            keys = jnp.concatenate([kv[n, :, pl.ds(0, HEAD)] for n in held], axis=0)
            score[k] = lax.dot_general(keys, query, (((1,), (1,)), ((), ())), preferred_element_type=F32)
            for j in range(WINDOW_BLOCKS):
                allowed = ahead >= -j * BLK
                if j == WINDOW_BLOCKS - 1:
                    allowed = allowed & causal
                v = jnp.where(allowed, score[k, pl.ds(j * BLK, BLK), :], NEG)
                score[k, pl.ds(j * BLK, BLK), :] = v
                largest = jnp.maximum(largest, v)
            largest = jnp.max(largest, axis=0, keepdims=True)
            total = jnp.zeros((BLK, BLK), F32)
            parts = []
            for j in range(WINDOW_BLOCKS):
                w = jnp.exp2(score[k, pl.ds(j * BLK, BLK), :] - largest)
                total = total + w
                parts.append(w.astype(BF16))
            weights = jnp.concatenate(parts, axis=0)
            values = jnp.concatenate([kv[n, :, pl.ds(HEAD, HEAD)] for n in held], axis=1)
            mixed = jnp.dot(values, weights, preferred_element_type=F32)
            mixed = (mixed / jnp.sum(total, axis=0, keepdims=True)).T.astype(BF16)
            t, h = UNITS[u]
            if t == 0:
                att[z, c, x, pl.ds(h * HALF + i * BLK, BLK), :] = mixed
            else:
                away[u - 2, pl.ds(i * BLK, BLK), :] = mixed

    home, lifts, relays = {}, {}, {}

    def source(t):
        return (x + 4 - SHIFT[t]) % 4

    def part_of(u):
        return pl.ds(UNITS[u][1] * HALF, HALF)

    def hop(u):
        home[u] = go.start(away.at[u - 2], att.at[z, c, x, part_of(u)], dx=SHIFT[UNITS[u][0]])

    def lift(u):
        if u in home:
            home[u].wait_recv()
        piece = att.at[z, c, source(UNITS[u][0]), part_of(u)]
        if u >= 6:
            relays[u] = go.start(piece, piece, dz=2)
        lifts[u] = go.start(piece, piece, dz=1), go.start(piece, piece, dz=3)

    def relay(u):
        t, h = UNITS[u]
        lifts[u][h].wait_recv()
        piece = att.at[(z + (1 if h else 3)) % 4, c, source(t), part_of(u)]
        relays[u] = go.start(piece, piece, dz=3 if h else 1)

    shared = {}

    def share(r, t):
        piece = att.at[(z + r) % 4, c, source(t)]
        shared[r, t] = go.start(piece, piece, dc=1)

    def units_of(t):
        return [u for u in range(8) if UNITS[u][0] == t]

    def settle(t):
        for u in units_of(t):
            lifts[u][1 - UNITS[u][1]].wait_recv()
            if u >= 6:
                lifts[u][UNITS[u][1]].wait_recv()
        share(3, t)
        share(1, t)
        for u in units_of(t):
            relays[u].wait_recv()
        share(2, t)

    def product(pieces, cols):
        left = jnp.concatenate([att[d, k, source(t)] for d, t in pieces for k in range(2)], axis=1)
        right = jnp.concatenate(
            [wo[pl.ds(pl.multiple_of((4 * d + source(t)) * 256, 256), 256), cols] for d, t in pieces], axis=0
        )
        return jnp.dot(left, right, preferred_element_type=F32)

    def multiply(pieces, first):
        def tile(n, carry):
            cols = pl.ds(pl.multiple_of(n * 256, 256), 256)
            part = product(pieces, cols)
            acc[:, cols] = part if first else acc[:, cols] + part
            return carry

        lax.fori_loop(0, 4, tile, 0, unroll=2)

    def bring(r, ts):
        for t in ts:
            shared[r, t].wait_recv()

    row = lambda r: blocks(r, 0, 4)
    kv_sib, kv_rel = [], []

    def kv_pass(r):
        up = r % 2 == 0
        kv_y[r][0 if up else 1].wait_recv()
        piece = blocks(3 if up else 1, (x + 4 - r) % 4, 1)
        kv_rel.append(go.start(piece, piece, dy=1 if up else 3))

    w_rel_up.wait_recv()
    w_rel_dn.wait_recv()
    sib0 = project(0, tok.at[top])
    for r in (1, 3):
        kv_x[r].wait_recv()
        kv_y[r] = kv_along_y(r)
    t_up_l = go.start(tok_hbm.at[low], tx.at[0, low], dx=1)
    t_dn_t = go.start(tok_hbm.at[top], tx.at[1, top], dx=3)
    kv_x[2].wait_recv()
    kv_y[2] = kv_along_y(2)
    kv_sib.append(go.start(row(0), row(0), dc=1))
    sib1 = project(1, tok.at[low])
    spread0 = spread(0, sib0)
    kv_pass(0)
    kv_pass(1)
    t_up_t.wait_recv()
    sib2 = project(2, tx.at[0, top])
    spread1 = spread(1, sib1)
    t_dn_l.wait_recv()
    t_rel_up = go.start(tx.at[0, top], tx.at[2, top], dx=1)
    t_rel_dn = go.start(tx.at[1, low], tx.at[2, low], dx=3)
    sib3 = project(3, tx.at[1, low])
    spread2 = spread(2, sib2)
    kv_pass(3)
    spread3 = spread(3, sib3)
    kv_pass(2)
    finish(0, spread0)
    finish(1, spread1)
    for r in range(4):
        kv_y[r][1 if r % 2 == 0 else 0].wait_recv()
    kv_sib.append(go.start(row(3), row(3), dc=1))
    kv_sib.append(go.start(row(1), row(1), dc=1))
    t_up_l.wait_recv()
    sib4 = project(4, tx.at[0, low])
    t_dn_t.wait_recv()
    sib5 = project(5, tx.at[1, top])
    finish(2, spread2)
    finish(3, spread3)
    for copy in kv_rel:
        copy.wait_recv()
    kv_sib.append(go.start(row(2), row(2), dc=1))
    spread4 = spread(4, sib4)
    spread5 = spread(5, sib5)
    for copy in kv_sib:
        copy.wait_recv()
    attend((0, 1))
    lift(0)
    lift(1)
    share(0, 0)
    t_rel_up.wait_recv()
    sib6 = project(6, tx.at[2, top])
    t_rel_dn.wait_recv()
    sib7 = project(7, tx.at[2, low])
    spread6 = spread(6, sib6)
    spread7 = spread(7, sib7)
    attend((2, 3))
    hop(2)
    hop(3)
    relay(0)
    relay(1)
    finish(4, spread4)
    finish(5, spread5)
    attend((4, 5))
    hop(4)
    hop(5)
    lift(2)
    lift(3)
    finish(6, spread6)
    finish(7, spread7)
    attend((6, 7))
    hop(6)
    hop(7)
    lift(4)
    lift(5)
    share(0, 1)
    share(0, 2)
    relay(2)
    relay(3)
    lift(6)
    lift(7)
    share(0, 3)
    settle(0)
    loads[4].wait()
    for r in range(4):
        bring(r, (0,))
    multiply([(d, 0) for d in range(4)], True)
    relay(4)
    relay(5)
    settle(1)
    for r in range(4):
        bring(r, (1,))
    multiply([(d, 1) for d in range(4)], False)
    settle(2)
    for r in range(4):
        bring(r, (2,))
    multiply([(d, 2) for d in range(4)], False)
    settle(3)
    for r in range(4):
        bring(r, (3,))
    last = [(d, 3) for d in range(4)]

    def close(n, carry):
        cols = pl.ds(pl.multiple_of(n * 256, 256), 256)
        out[:, cols] = (acc[:, cols] + product(last, cols)).astype(BF16)
        return carry

    lax.fori_loop(0, 4, close, 0, unroll=2)
    go.drain()


def layer(order, lengths, tok, wq, wkv, wo):
    vm = pl.BlockSpec(memory_space=pltpu.VMEM)
    sm = pl.BlockSpec(memory_space=pltpu.SMEM)
    hbm = pl.BlockSpec(memory_space=pl.ANY)
    n = 136
    return pl.pallas_call(
        layer_kernel,
        out_shape=jax.ShapeDtypeStruct((ROWS, WIDTH), BF16),
        in_specs=[sm] * 2 + [hbm] * 5,
        out_specs=vm,
        scratch_shapes=[
            pltpu.VMEM((3 * BLK, HEAD), F32),
            pltpu.VMEM((ROWS, WIDTH), BF16),
            pltpu.VMEM((WIDTH, WIDTH), BF16),
            pltpu.VMEM((4 * WIDTH, WIDTH), BF16),
            pltpu.VMEM((3, ROWS, WIDTH), BF16),
            pltpu.VMEM((4, WIDTH, 256), BF16),
            pltpu.VMEM((64, BLK, 256), BF16),
            pltpu.VMEM((4, 256, 256), F32),
            pltpu.VMEM((4, 256, 256), BF16),
            pltpu.VMEM((4, 256, 256), BF16),
            pltpu.VMEM((3, 256, 256), BF16),
            pltpu.VMEM((3, 256, 256), BF16),
            pltpu.VMEM((8, 4, HALF, HEAD), F32),
            pltpu.VMEM((8, 4, HALF, HEAD), BF16),
            pltpu.VMEM((8, 4, HALF, HEAD), BF16),
            pltpu.VMEM((8, 3, HALF, HEAD), BF16),
            pltpu.VMEM((8, 3, HALF, HEAD), BF16),
            pltpu.VMEM((8, HALF, HEAD), BF16),
            pltpu.VMEM((4, WINDOW_BLOCKS * BLK, BLK), F32),
            pltpu.VMEM((6, HALF, HEAD), BF16),
            pltpu.VMEM((4, 2, 4, ROWS, HEAD), BF16),
            pltpu.VMEM((ROWS, WIDTH), F32),
            pltpu.VMEM((16, BLK), jnp.int32),
            pltpu.SMEM((16, BLK), jnp.int32),
            pltpu.SemaphoreType.DMA((6,)),
            pltpu.SemaphoreType.DMA((n,)),
            pltpu.SemaphoreType.DMA((n,)),
        ],
        compiler_params=pltpu.CompilerParams(
            collective_id=0, has_side_effects=True, vmem_limit_bytes=54 << 20
        ),
    )(order, lengths, jnp.asarray(rope_tables()), tok, wq, wkv, wo)


def body(tokens, query_weight, key_value_matrix, output_weight, document_lengths, block_order):
    return layer(
        block_order, document_lengths, tokens, query_weight, key_value_matrix, output_weight
    )


def solution(mesh):
    placed = (P("seq", "mp"), P("mp", "seq"), P("mp", None), P(None, "mp"), P(), P())
    return jax.shard_map(
        body, mesh=mesh, in_specs=placed, out_specs=P("seq", "mp"), check_vma=False
    )
```

```python
import functools
import math

import jax
import jax.numpy as jnp
import numpy as np
from jax import lax
from jax.experimental import pallas as pl
from jax.experimental.pallas import tpu as pltpu
from jax.sharding import PartitionSpec as P

MESH = pl.DeviceIdType.MESH
HEAD = 128
BLK = 128
ROWS = 512
WIDTH = 1024
WINDOW_BLOCKS = 17
ROPE_BASE = 500000.0
NEG = -1e30
BF16 = jnp.bfloat16
F32 = jnp.float32


UNITS = ((0, 0), (0, 1), (1, 0), (2, 1), (1, 1), (2, 0), (3, 0), (3, 1))
SHIFT = (0, 3, 1, 2)
HALF = ROWS // 2


def rope_tables():
    half = HEAD // 2
    inverse = np.exp(-(2.0 * np.arange(half) / HEAD) * np.log(ROPE_BASE))
    within = np.arange(BLK)[:, None] * inverse[None, :]
    start = (np.arange(64) * BLK)[:, None] * inverse[None, :]

    def both(values, sign):
        return np.concatenate([sign * values, values], axis=1).astype(np.float32)

    return np.concatenate(
        [
            both(np.cos(within), 1.0),
            both(np.sin(within), -1.0),
            both(np.cos(start), 1.0),
            both(np.sin(start), -1.0),
        ]
    )


def place():
    s = lax.axis_index("seq")
    m = lax.axis_index("mp")
    return s // 4, s % 4, m // 2, m % 2


def at(y, x, z, c, dy=0, dx=0, dz=0, dc=0):
    return (((y + dy) % 4) * 4 + (x + dx) % 4, ((z + dz) % 4) * 2 + (c + dc) % 2)


def greet(here, offsets):
    barrier = pltpu.get_barrier_semaphore()
    for off in offsets:
        pl.semaphore_signal(barrier, inc=1, device_id=at(*here, **off), device_id_type=MESH)
    pl.semaphore_wait(barrier, len(offsets))


class Copies:
    def __init__(self, here, send, recv):
        self.here, self.send, self.recv = here, send, recv
        self.count, self.open = 0, []

    def start(self, src, dst, **off):
        k = self.count
        self.count += 1
        copy = pltpu.make_async_remote_copy(
            src_ref=src,
            dst_ref=dst,
            send_sem=self.send.at[k],
            recv_sem=self.recv.at[k],
            device_id=at(*self.here, **off),
            device_id_type=MESH,
        )
        copy.start()
        self.open.append(copy)
        return copy

    def drain(self):
        for copy in self.open:
            copy.wait_send()


def turn(values, block, table):
    cr, sr = table[pl.ds(0, BLK), :], table[pl.ds(BLK, BLK), :]
    c0 = table[pl.ds(2 * BLK + block, 1), :]
    s0 = table[pl.ds(2 * BLK + 64 + block, 1), :]
    cosine = c0 * cr - s0 * sr
    sine = s0 * cr + c0 * sr
    return values * cosine + pltpu.roll(values, HEAD // 2, 1) * sine


OFFSETS = [
    dict(dx=1),
    dict(dx=3),
    dict(dx=2),
    dict(dy=1),
    dict(dy=3),
    dict(dz=1),
    dict(dz=3),
    dict(dz=2),
    dict(dc=1),
]


def layer_kernel(
    order, lengths, table_hbm, tok_hbm, wq, wkv_hbm, wo_hbm, out,
    table, tok, wkv, wo, tx, wy, kv, kv_mine, kv_sib_s, kv_sib_r, kv_z_s, kv_z_r,
    q_mine, q_sib_s, q_sib_r, q_z_s, q_z_r, q, score, away, att, acc, windows, where, local, send, recv,
):
    here = place()
    y, x, z, c = here
    s = 4 * y + x
    loads = [
        pltpu.make_async_copy(src, dst, local.at[k])
        for k, (src, dst) in enumerate(
            ((tok_hbm, tok), (wkv_hbm, wkv), (table_hbm, table), (wq, wy.at[y]), (wo_hbm, wo))
        )
    ]
    for load in loads[:4]:
        load.start()
    greet(here, OFFSETS)
    go = Copies(here, send, recv)
    top, low = pl.ds(0, HALF), pl.ds(HALF, HALF)
    wtop, wlow = pl.ds(0, WIDTH // 2), pl.ds(WIDTH // 2, WIDTH // 2)

    t_up_t = go.start(tok_hbm.at[top], tx.at[0, top], dx=1)
    t_dn_l = go.start(tok_hbm.at[low], tx.at[1, low], dx=3)
    w_up_t = go.start(wq.at[wtop], wy.at[y, wtop], dy=1)
    w_dn_l = go.start(wq.at[wlow], wy.at[y, wlow], dy=3)
    w_up_l = go.start(wq.at[wlow], wy.at[y, wlow], dy=1)
    w_dn_t = go.start(wq.at[wtop], wy.at[y, wtop], dy=3)

    def pair_part(half, into):
        rows = tok[pl.ds(pl.multiple_of(half * HALF, HALF), HALF), :]
        for g in range(4):
            part = jnp.dot(rows, wkv[:, pl.ds(g * 256, 256)], preferred_element_type=F32)
            for i in range(2):
                h = 2 * g + i
                into[h % 4, :, pl.ds((h // 4) * HEAD, HEAD)] = part[:, i * HEAD : (i + 1) * HEAD].astype(into.dtype)

    loads[0].wait()
    loads[1].wait()
    pair_part(1 - c, kv_sib_s)
    sib = go.start(kv_sib_s, kv_sib_r, dc=1)
    pair_part(c, kv_mine)
    sib.wait_recv()
    kv_z = []
    for r in (2, 1, 3):
        d = (z + r) % 4
        kv_z_s[r - 1] = (kv_mine[d] + kv_sib_r[d].astype(F32)).astype(BF16)
        kv_z.append(go.start(kv_z_s.at[r - 1], kv_z_r.at[r - 1], dz=r))
    loads[4].start()
    lane = lax.broadcasted_iota(jnp.int32, (16, BLK), 1)
    line = lax.broadcasted_iota(jnp.int32, (16, BLK), 0)
    wanted = lane - (WINDOW_BLOCKS - 1)
    for n in range(16):
        t, h = UNITS[n // 2]
        mine = order[4 * (4 * y + (x + SHIFT[t]) % 4) + 2 * h + n % 2]
        wanted = wanted + jnp.where(line == n, mine, 0)
    wanted = jnp.maximum(wanted, 0)
    found = jnp.zeros((16, BLK), jnp.int32)
    for n in range(64):
        found = jnp.where(wanted == order[n], n % 4 // 2 * 32 + n // 4 * 2 + n % 2, found)
    windows[...] = found
    table_copy = pltpu.make_async_copy(windows, where, local.at[5])
    table_copy.start()
    loads[2].wait()
    loads[3].wait()
    table_copy.wait()
    w_up_t.wait_recv()
    piece = wy.at[(y + 3) % 4, wtop]
    w_rel_up = go.start(piece, piece, dy=1)
    w_dn_l.wait_recv()
    piece = wy.at[(y + 1) % 4, wlow]
    w_rel_dn = go.start(piece, piece, dy=3)
    w_up_l.wait_recv()
    w_dn_t.wait_recv()
    for copy in kv_z:
        copy.wait_recv()
    own_pair = kv_mine[z] + kv_sib_r[z].astype(F32)
    for r in range(3):
        own_pair = own_pair + kv_z_r[r].astype(F32)
    for i in range(2):
        part = own_pair[i * BLK : (i + 1) * BLK]
        kv[32 * c + 2 * s + i, :, pl.ds(0, HEAD)] = turn(part[:, :HEAD], order[4 * s + 2 * c + i], table).astype(BF16)
        kv[32 * c + 2 * s + i, :, pl.ds(HEAD, HEAD)] = part[:, HEAD:].T.astype(BF16)

    def blocks(dy, column, n):
        return kv.at[pl.ds(32 * c + 8 * ((y + dy) % 4) + 2 * column, 2 * n)]

    own = blocks(0, x, 1)
    kv_x = {r: go.start(own, own, dx=r) for r in (1, 3, 2)}

    def kv_along_y(r):
        piece = blocks(0, (x + 4 - r) % 4, 1)
        return go.start(piece, piece, dy=1), go.start(piece, piece, dy=3)

    kv_y = {0: kv_along_y(0)}

    def project(u, rows_ref):
        def one(g, carry):
            part = jnp.dot(rows_ref[...], wy[g], preferred_element_type=F32)
            first, second = part[:, :HEAD], part[:, HEAD:]
            q_mine[u, g] = jnp.where(c == 0, first, second)
            q_sib_s[u, g] = jnp.where(c == 0, second, first).astype(BF16)
            return carry

        lax.fori_loop(0, 4, one, 0, unroll=4)
        return go.start(q_sib_s.at[u], q_sib_r.at[u], dc=1)

    def spread(u, copy):
        copy.wait_recv()
        sent = []
        for r in (2, 1, 3):
            d = (z + r) % 4
            q_z_s[u, r - 1] = (q_mine[u, d] + q_sib_r[u, d].astype(F32)).astype(BF16)
            sent.append(go.start(q_z_s.at[u, r - 1], q_z_r.at[u, r - 1], dz=r))
        return sent

    scale = math.log2(math.e) / math.sqrt(HEAD)

    def spot_of(u, i):
        t, h = UNITS[u]
        return 4 * (4 * y + (x + SHIFT[t]) % 4) + 2 * h + i

    def block_at(u, i):
        return order[spot_of(u, i)]

    def finish(u, sent):
        for copy in sent:
            copy.wait_recv()
        for i in range(2):
            rows = pl.ds(i * BLK, BLK)
            total = q_mine[u, z, rows, :] + q_sib_r[u, z, rows, :].astype(F32)
            for r in range(3):
                total = total + q_z_r[u, r, rows, :].astype(F32)
            q[u, rows, :] = (turn(total, block_at(u, i), table) * scale).astype(BF16)

    def attend(units):
        for k, (u, i) in enumerate([(u, i) for u in units for i in range(2)]):
            block = block_at(u, i)
            query = q[u, pl.ds(i * BLK, BLK), :]
            pos = lax.broadcasted_iota(jnp.int32, (1, BLK), 1) + block * BLK
            begin = jnp.zeros((1, BLK), jnp.int32)
            end = jnp.int32(0)
            for d in range(16):
                end = end + lengths[d]
                begin = jnp.where(pos >= end, end, begin)
            row = lax.broadcasted_iota(jnp.int32, (BLK, BLK), 0)
            ahead = row - (begin - (block - (WINDOW_BLOCKS - 1)) * BLK)
            causal = row <= lax.broadcasted_iota(jnp.int32, (BLK, BLK), 1)
            largest = jnp.full((BLK, BLK), NEG, F32)
            held = [where[2 * u + i, j] for j in range(WINDOW_BLOCKS)]
            keys = jnp.concatenate([kv[n, :, pl.ds(0, HEAD)] for n in held], axis=0)
            score[k] = lax.dot_general(keys, query, (((1,), (1,)), ((), ())), preferred_element_type=F32)
            for j in range(WINDOW_BLOCKS):
                allowed = ahead >= -j * BLK
                if j == WINDOW_BLOCKS - 1:
                    allowed = allowed & causal
                v = jnp.where(allowed, score[k, pl.ds(j * BLK, BLK), :], NEG)
                score[k, pl.ds(j * BLK, BLK), :] = v
                largest = jnp.maximum(largest, v)
            largest = jnp.max(largest, axis=0, keepdims=True)
            total = jnp.zeros((BLK, BLK), F32)
            parts = []
            for j in range(WINDOW_BLOCKS):
                w = jnp.exp2(score[k, pl.ds(j * BLK, BLK), :] - largest)
                total = total + w
                parts.append(w.astype(BF16))
            weights = jnp.concatenate(parts, axis=0)
            values = jnp.concatenate([kv[n, :, pl.ds(HEAD, HEAD)] for n in held], axis=1)
            mixed = jnp.dot(values, weights, preferred_element_type=F32)
            mixed = (mixed / jnp.sum(total, axis=0, keepdims=True)).T.astype(BF16)
            t, h = UNITS[u]
            if t == 0:
                att[z, c, x, pl.ds(h * HALF + i * BLK, BLK), :] = mixed
            else:
                away[u - 2, pl.ds(i * BLK, BLK), :] = mixed

    home, lifts, relays = {}, {}, {}

    def source(t):
        return (x + 4 - SHIFT[t]) % 4

    def part_of(u):
        return pl.ds(UNITS[u][1] * HALF, HALF)

    def hop(u):
        home[u] = go.start(away.at[u - 2], att.at[z, c, x, part_of(u)], dx=SHIFT[UNITS[u][0]])

    def lift(u):
        if u in home:
            home[u].wait_recv()
        piece = att.at[z, c, source(UNITS[u][0]), part_of(u)]
        if u >= 6:
            relays[u] = go.start(piece, piece, dz=2)
        lifts[u] = go.start(piece, piece, dz=1), go.start(piece, piece, dz=3)

    def relay(u):
        t, h = UNITS[u]
        lifts[u][h].wait_recv()
        piece = att.at[(z + (1 if h else 3)) % 4, c, source(t), part_of(u)]
        relays[u] = go.start(piece, piece, dz=3 if h else 1)

    shared = {}

    def share(r, t):
        piece = att.at[(z + r) % 4, c, source(t)]
        shared[r, t] = go.start(piece, piece, dc=1)

    def units_of(t):
        return [u for u in range(8) if UNITS[u][0] == t]

    def settle(t):
        for u in units_of(t):
            lifts[u][1 - UNITS[u][1]].wait_recv()
            if u >= 6:
                lifts[u][UNITS[u][1]].wait_recv()
        share(3, t)
        share(1, t)
        for u in units_of(t):
            relays[u].wait_recv()
        share(2, t)

    def product(pieces, cols):
        left = jnp.concatenate([att[d, k, source(t)] for d, t in pieces for k in range(2)], axis=1)
        right = jnp.concatenate(
            [wo[pl.ds(pl.multiple_of((4 * d + source(t)) * 256, 256), 256), cols] for d, t in pieces], axis=0
        )
        return jnp.dot(left, right, preferred_element_type=F32)

    def multiply(pieces, first):
        def tile(n, carry):
            cols = pl.ds(pl.multiple_of(n * 256, 256), 256)
            part = product(pieces, cols)
            acc[:, cols] = part if first else acc[:, cols] + part
            return carry

        lax.fori_loop(0, 4, tile, 0, unroll=4)

    def bring(r, ts):
        for t in ts:
            shared[r, t].wait_recv()

    row = lambda r: blocks(r, 0, 4)
    kv_sib, kv_rel = [], []

    def kv_pass(r):
        up = r % 2 == 0
        kv_y[r][0 if up else 1].wait_recv()
        piece = blocks(3 if up else 1, (x + 4 - r) % 4, 1)
        kv_rel.append(go.start(piece, piece, dy=1 if up else 3))

    w_rel_up.wait_recv()
    w_rel_dn.wait_recv()
    sib0 = project(0, tok.at[top])
    for r in (1, 3):
        kv_x[r].wait_recv()
        kv_y[r] = kv_along_y(r)
    t_up_l = go.start(tok_hbm.at[low], tx.at[0, low], dx=1)
    t_dn_t = go.start(tok_hbm.at[top], tx.at[1, top], dx=3)
    kv_x[2].wait_recv()
    kv_y[2] = kv_along_y(2)
    kv_sib.append(go.start(row(0), row(0), dc=1))
    sib1 = project(1, tok.at[low])
    spread0 = spread(0, sib0)
    kv_pass(0)
    kv_pass(1)
    t_up_t.wait_recv()
    sib2 = project(2, tx.at[0, top])
    spread1 = spread(1, sib1)
    t_dn_l.wait_recv()
    t_rel_up = go.start(tx.at[0, top], tx.at[2, top], dx=1)
    t_rel_dn = go.start(tx.at[1, low], tx.at[2, low], dx=3)
    sib3 = project(3, tx.at[1, low])
    spread2 = spread(2, sib2)
    kv_pass(3)
    spread3 = spread(3, sib3)
    kv_pass(2)
    finish(0, spread0)
    finish(1, spread1)
    for r in range(4):
        kv_y[r][1 if r % 2 == 0 else 0].wait_recv()
    kv_sib.append(go.start(row(3), row(3), dc=1))
    kv_sib.append(go.start(row(1), row(1), dc=1))
    t_up_l.wait_recv()
    sib4 = project(4, tx.at[0, low])
    t_dn_t.wait_recv()
    sib5 = project(5, tx.at[1, top])
    finish(2, spread2)
    finish(3, spread3)
    for copy in kv_rel:
        copy.wait_recv()
    kv_sib.append(go.start(row(2), row(2), dc=1))
    spread4 = spread(4, sib4)
    spread5 = spread(5, sib5)
    for copy in kv_sib:
        copy.wait_recv()
    attend((0, 1))
    lift(0)
    lift(1)
    share(0, 0)
    t_rel_up.wait_recv()
    sib6 = project(6, tx.at[2, top])
    t_rel_dn.wait_recv()
    sib7 = project(7, tx.at[2, low])
    spread6 = spread(6, sib6)
    spread7 = spread(7, sib7)
    attend((2, 3))
    hop(2)
    hop(3)
    relay(0)
    relay(1)
    finish(4, spread4)
    finish(5, spread5)
    attend((4, 5))
    hop(4)
    hop(5)
    lift(2)
    lift(3)
    finish(6, spread6)
    finish(7, spread7)
    attend((6, 7))
    hop(6)
    hop(7)
    lift(4)
    lift(5)
    share(0, 1)
    share(0, 2)
    relay(2)
    relay(3)
    lift(6)
    lift(7)
    share(0, 3)
    settle(0)
    loads[4].wait()
    for r in range(4):
        bring(r, (0,))
    multiply([(d, 0) for d in range(4)], True)
    relay(4)
    relay(5)
    settle(1)
    for r in range(4):
        bring(r, (1,))
    multiply([(d, 1) for d in range(4)], False)
    settle(2)
    for r in range(4):
        bring(r, (2,))
    multiply([(d, 2) for d in range(4)], False)
    settle(3)
    for r in range(4):
        bring(r, (3,))
    last = [(d, 3) for d in range(4)]

    def close(n, carry):
        cols = pl.ds(pl.multiple_of(n * 256, 256), 256)
        out[:, cols] = (acc[:, cols] + product(last, cols)).astype(BF16)
        return carry

    lax.fori_loop(0, 4, close, 0, unroll=4)
    go.drain()


def layer(order, lengths, tok, wq, wkv, wo):
    vm = pl.BlockSpec(memory_space=pltpu.VMEM)
    sm = pl.BlockSpec(memory_space=pltpu.SMEM)
    hbm = pl.BlockSpec(memory_space=pl.ANY)
    n = 136
    return pl.pallas_call(
        layer_kernel,
        out_shape=jax.ShapeDtypeStruct((ROWS, WIDTH), BF16),
        in_specs=[sm] * 2 + [hbm] * 5,
        out_specs=vm,
        scratch_shapes=[
            pltpu.VMEM((3 * BLK, HEAD), F32),
            pltpu.VMEM((ROWS, WIDTH), BF16),
            pltpu.VMEM((WIDTH, WIDTH), BF16),
            pltpu.VMEM((4 * WIDTH, WIDTH), BF16),
            pltpu.VMEM((3, ROWS, WIDTH), BF16),
            pltpu.VMEM((4, WIDTH, 256), BF16),
            pltpu.VMEM((64, BLK, 256), BF16),
            pltpu.VMEM((4, 256, 256), F32),
            pltpu.VMEM((4, 256, 256), BF16),
            pltpu.VMEM((4, 256, 256), BF16),
            pltpu.VMEM((3, 256, 256), BF16),
            pltpu.VMEM((3, 256, 256), BF16),
            pltpu.VMEM((8, 4, HALF, HEAD), F32),
            pltpu.VMEM((8, 4, HALF, HEAD), BF16),
            pltpu.VMEM((8, 4, HALF, HEAD), BF16),
            pltpu.VMEM((8, 3, HALF, HEAD), BF16),
            pltpu.VMEM((8, 3, HALF, HEAD), BF16),
            pltpu.VMEM((8, HALF, HEAD), BF16),
            pltpu.VMEM((4, WINDOW_BLOCKS * BLK, BLK), F32),
            pltpu.VMEM((6, HALF, HEAD), BF16),
            pltpu.VMEM((4, 2, 4, ROWS, HEAD), BF16),
            pltpu.VMEM((ROWS, WIDTH), F32),
            pltpu.VMEM((16, BLK), jnp.int32),
            pltpu.SMEM((16, BLK), jnp.int32),
            pltpu.SemaphoreType.DMA((6,)),
            pltpu.SemaphoreType.DMA((n,)),
            pltpu.SemaphoreType.DMA((n,)),
        ],
        compiler_params=pltpu.CompilerParams(
            collective_id=0, has_side_effects=True, vmem_limit_bytes=54 << 20
        ),
    )(order, lengths, jnp.asarray(rope_tables()), tok, wq, wkv, wo)


def body(tokens, query_weight, key_value_matrix, output_weight, document_lengths, block_order):
    return layer(
        block_order, document_lengths, tokens, query_weight, key_value_matrix, output_weight
    )


def solution(mesh):
    placed = (P("seq", "mp"), P("mp", "seq"), P("mp", None), P(None, "mp"), P(), P())
    return jax.shard_map(
        body, mesh=mesh, in_specs=placed, out_specs=P("seq", "mp"), check_vma=False
    )
```
